128 devices in a mesh: lat: 32 (over z, x_hi, y), lon: 4 (over x_lo, core).
Axes of the slice: x: 4 (x_hi: 2, x_lo: 2; x = x_hi * 2 + x_lo), y: 4, z: 4, core: 2. Of those that a mesh axis runs over, the one named last changes fastest.
Arguments:
- height: float32 [4352, 9216], P('lat', 'lon'), may hold values from -6 to 6
- flux_east: float32 [4352, 9216], P('lat', 'lon'), may hold values from -4 to 4
- flux_north: float32 [4352, 9216], P('lat', 'lon'), may hold values from -4 to 4
- bathymetry: float32 [4352, 9216], P('lat', 'lon'), may hold values from -1 to 4
- wet_mask: int32 [4352, 9216], P('lat', 'lon'), may hold values 0 or 1
- wavenumber: int32 [32], replicated, may hold values from 0 to 4351, as said below
- legendre: bfloat16 [32, 4352, 4608], P('lat', None, 'lon'), may hold values from -0.0625 to 0.0625
- quadrature: float32 [4352], replicated, may hold values from 0.5 to 2
- love_factor: float32 [4608], P('lon'), may hold values from 0.2 to 1
Outputs:
- new_height: float32 [4352, 9216], P('lat', 'lon')
- new_east: float32 [4352, 9216], P('lat', 'lon')
- new_north: float32 [4352, 9216], P('lat', 'lon')
The draws below stay inside these ranges and needn't reach their ends.
Inputs may be any that keep to these rules, and one draw needn't show every extreme that they name: `wavenumber`: the 32 values are distinct; 0 and 4351 are always among them.
All inputs are finite; a program needn't handle non-finite values. No bound on the sum of `wet_mask` on one device may be relied on, other than what follows from the above.
Results may differ from the reference program's by a relative error of at most 0.0003.
Values sent between devices are 32-bit elements; how exact they have to be, the bound alone decides.
No kernel may reach another device: no remote copies, remote signals or barrier semaphores. Data moves between devices by JAX's collectives and lax.ppermute only.
A program may use at most 128 MiB of HBM per device.

```python
import math
import jax
import jax.numpy as jnp
from jax import lax

NLAT = 4352
NLON = 9216
NDEG = 4608
STEPS = 12
M_TOT = 32


def draw_wavenumber(key, part):
    key = jax.random.fold_in(key, 11)
    first_key, second_key = jax.random.split(key)
    inner = jax.random.permutation(first_key, NLAT - 2).astype(jnp.int32) + 1
    chosen = jnp.concatenate([jnp.array([0, NLAT - 1], jnp.int32), inner[:M_TOT - 2]])
    return jax.random.permutation(second_key, chosen).astype(jnp.int32)


def set_ends(result, key, least, high):
    longest = result.shape.index(max(result.shape))
    spots = []
    for shift in (0, 1):
        where = [jax.random.randint(jax.random.fold_in(key, axis), (), 0, length) for axis, length in enumerate(result.shape)]
        where[longest] = (where[longest] + shift) % result.shape[longest]
        spots.append(tuple(where))
    return result.at[spots[0]].set(least).at[spots[1]].set(high)


def shard_levels(stream_key, dims, pieces, low, high):
    level = 1.0
    for position, shards_of in pieces:
        heights = jax.random.uniform(jax.random.fold_in(jax.random.fold_in(stream_key, 6), position), (shards_of,), jnp.float32, low / len(pieces), high / len(pieces))
        level = level * jnp.repeat(jnp.exp(heights), dims[position] // shards_of).reshape((-1,) + (1,) * (len(dims) - 1 - position))
    return level


def normal_values(rng, shape, deviation, bound, shards=(), kind=jnp.bfloat16):
    entries = deviation * jax.random.normal(rng, shape, jnp.float32)
    if shards:
        entries = entries * shard_levels(rng, shape, shards, -0.22, 0.18)
    return jnp.clip(entries, -bound, bound).astype(kind)


def setup_inputs(seed: int = 0) -> dict:
    seeds = jax.random.split(jax.random.key(seed), 10)
    height = normal_values(seeds[0], (NLAT, NLON), 1.0, 6.0, ((0, 32), (1, 4)), jnp.float32)
    flux_east = normal_values(seeds[1], (NLAT, NLON), 0.5, 4.0, ((0, 32), (1, 4)), jnp.float32)
    flux_north = normal_values(seeds[2], (NLAT, NLON), 0.5, 4.0, ((0, 32), (1, 4)), jnp.float32)
    bathymetry = jnp.clip(-1.0 + 5.0 * jax.random.uniform(seeds[3], (NLAT, NLON), jnp.float32) ** shard_levels(seeds[3], (NLAT, NLON), ((0, 32), (1, 4)), -0.2, 0.2), -1.0, 4.0)
    wet_mask = set_ends((jax.random.randint(seeds[4], (NLAT, NLON), 0, 8) < 7).astype(jnp.int32), jax.random.fold_in(seeds[4], 1), 0, 1)
    wavenumber = draw_wavenumber(jax.random.fold_in(seeds[9], 71), 0)
    legendre = normal_values(seeds[6], (M_TOT, NLAT, NDEG), (NLAT + NDEG) ** -0.5, 0.0625, ((0, 32), (2, 4)))
    quadrature = jnp.clip(jnp.exp(jax.random.uniform(seeds[7], (NLAT,), jnp.float32, math.log(0.5), math.log(2.0))), 0.5, 2.0)
    love_factor = jnp.clip(0.2 + 0.8 * jax.random.uniform(seeds[8], (NDEG,), jnp.float32) ** shard_levels(seeds[8], (NDEG,), ((0, 4),), -0.2, 0.2), 0.2, 1.0)
    return dict(height=height, flux_east=flux_east, flux_north=flux_north, bathymetry=bathymetry, wet_mask=wet_mask, wavenumber=wavenumber, legendre=legendre, quadrature=quadrature, love_factor=love_factor)


gravity_step = 0.12
volume_step = 0.12
retain_factor = 0.97

def basis_table(wavenumber):
    columns = jnp.arange(NLON, dtype=jnp.int32)
    product = wavenumber.astype(jnp.int32)[:, None] * columns[None, :] % NLON
    angle = product.astype(jnp.float32) * (2.0 * math.pi / NLON)
    return jnp.concatenate([jnp.cos(angle), -jnp.sin(angle)], axis=0)

def north_of(field):
    return jnp.concatenate([field[1:], jnp.zeros((1, field.shape[1]), jnp.float32)], axis=0)

def south_of(field):
    return jnp.concatenate([jnp.zeros((1, field.shape[1]), jnp.float32), field[:-1]], axis=0)

def reference(height, flux_east, flux_north, bathymetry, wet_mask, wavenumber, legendre, quadrature, love_factor):
    wetness = wet_mask.astype(jnp.float32)
    basis = basis_table(wavenumber)
    highest = lax.Precision.HIGHEST

    def advance(counter, carry):
        level, east, north = carry
        fourier = jnp.dot(basis, level.T, precision=highest) * (1.0 / math.sqrt(NLON))
        weighted = (fourier.reshape(2, M_TOT, NLAT) * quadrature).astype(jnp.bfloat16)

        def slot_work(index):
            table = legendre[index]
            coeff = jnp.dot(weighted[:, index, :], table, preferred_element_type=jnp.float32)
            scaled = (coeff * love_factor).astype(jnp.bfloat16)
            return jnp.dot(scaled, table.T, preferred_element_type=jnp.float32)
        back = lax.map(slot_work, jnp.arange(M_TOT, dtype=jnp.int32))
        back = jnp.transpose(back, (1, 0, 2)).reshape(2 * M_TOT, NLAT)
        attraction = jnp.dot(back.T, basis, precision=highest) * (1.0 / math.sqrt(NLON))
        potential = level + attraction
        column_depth = wetness * jnp.maximum(bathymetry + level, 0.0)
        potential_east = jnp.roll(potential, -1, axis=1)
        depth_east = jnp.roll(column_depth, -1, axis=1)
        wet_east = jnp.roll(wetness, -1, axis=1)
        potential_north = north_of(potential)
        depth_north = north_of(column_depth)
        wet_north = north_of(wetness)
        open_east = wetness * wet_east
        east_new = retain_factor * open_east * (east - gravity_step * 0.5 * (column_depth + depth_east) * open_east * (potential_east - potential))
        open_north = wetness * wet_north
        north_new = retain_factor * open_north * (north - gravity_step * 0.5 * (column_depth + depth_north) * open_north * (potential_north - potential))
        east_west = jnp.roll(east_new, 1, axis=1)
        north_south = south_of(north_new)
        level_new = level - volume_step * wetness * (east_new - east_west + north_new - north_south)
        return (level_new, east_new, north_new)
    final = lax.fori_loop(0, STEPS, advance, (height, flux_east, flux_north))
    return (final[0], final[1], final[2])
```

```python
import math

import jax
import jax.numpy as jnp
from jax import lax
from jax.experimental import pallas as pl
from jax.experimental.pallas import tpu as pltpu
from jax.sharding import PartitionSpec as P

STEPS = 12
HALO = STEPS
LANES = 128
MSG = 256

gravity_step = 0.12
volume_step = 0.12
retain_factor = 0.97

BOTH = ("lat", "lon")
VMEM = pl.BlockSpec(memory_space=pltpu.VMEM)
HIGH = jnp.float32
LOW = jnp.bfloat16


def in_vmem(value):
    return pltpu.with_memory_space_constraint(value, pltpu.VMEM)


def split_pair(value):
    high = value.astype(LOW)
    return high, (value - high.astype(HIGH)).astype(LOW)


def fourier_sums(rows, level_ref, table_ref, out_ref):
    cols = table_ref.shape[0]
    total = jnp.zeros((2 * rows, LANES), HIGH)
    for start in range(0, cols, 256):
        high, low = split_pair(level_ref[:rows, start : start + 256])
        both = jnp.concatenate([high, low], axis=0)
        total = total + jnp.dot(both, table_ref[start : start + 256, :], preferred_element_type=HIGH)
    half = total[:rows] + total[rows:]
    half = half + pltpu.roll(half, LANES // 2, 1)
    half = jnp.concatenate([half, jnp.zeros((MSG - rows, LANES), HIGH)], axis=0)
    sums = jnp.transpose(half)
    slots = out_ref.shape[0] // 4
    for slot in range(slots):
        pair = sums[2 * slot : 2 * slot + 2, :]
        for part in range(4):
            out_ref[4 * slot + part] = pair


def first_kernel(rows, level_ref, table_ref, out_ref):
    fourier_sums(rows, level_ref, table_ref, out_ref)


def grid_kernel(
    rows,
    got_ref,
    level_in,
    east_in,
    north_in,
    bathy_ref,
    wet_ref,
    east_open_ref,
    north_open_ref,
    synth_ref,
    table_ref,
    level_ref,
    east_ref,
    north_ref,
    out_ref,
    back_ref,
    pot_ref,
    depth_ref,
):
    tall, wide = level_in.shape
    slots = got_ref.shape[0] // 4
    for slot in range(slots):
        pair = got_ref[4 * slot]
        for part in range(1, 4):
            pair = pair + got_ref[4 * slot + part]
        back_ref[2 * slot : 2 * slot + 2, :] = pair
    back = back_ref[...] * (1.0 / math.sqrt(4 * table_ref.shape[0]))
    lane = lax.broadcasted_iota(jnp.int32, back.shape, 1)
    back = jnp.where(
        lane < tall - HALO, pltpu.roll(back, MSG - HALO, 1), pltpu.roll(back, tall - HALO, 1)
    )
    high, low = split_pair(back)
    high, low = high.astype(HIGH), low.astype(HIGH)
    stacked = jnp.concatenate([high, high, low, jnp.zeros_like(low)], axis=0)
    factors = jnp.transpose(stacked)[:tall].astype(LOW)
    half_gravity = gravity_step * 0.5
    for start in range(0, wide, 256):
        block = slice(start, min(start + 256, wide))
        pull = jnp.dot(factors, synth_ref[:, block], preferred_element_type=HIGH)
        level = level_in[:, block]
        pot_ref[:tall, block] = level + pull
        depth_ref[:tall, block] = (half_gravity * wet_ref[:, block]) * jnp.maximum(
            bathy_ref[:, block] + level, 0.0
        )
    pot_ref[tall:, :] = pot_ref[:8, :]
    depth_ref[tall:, :] = depth_ref[:8, :]

    def fluxes(start):
        here = slice(start, start + 8)
        above = slice(start + 1, start + 9)
        pot, depth = pot_ref[here, :], depth_ref[here, :]
        pot_east, depth_east = pltpu.roll(pot, wide - 1, 1), pltpu.roll(depth, wide - 1, 1)
        east_ref[here, :] = east_open_ref[here, :] * (
            east_in[here, :] - (depth + depth_east) * (pot_east - pot)
        )
        north_ref[here, :] = north_open_ref[here, :] * (
            north_in[here, :] - (depth + depth_ref[above, :]) * (pot_ref[above, :] - pot)
        )

    def levels(start):
        here = slice(start, start + 8)
        east, north = east_ref[here, :], north_ref[here, :]
        if start:
            below = north_ref[start - 1 : start + 7, :]
        else:
            below = jnp.concatenate([north_ref[tall - 1 :, :], north_ref[:7, :]], axis=0)
        level_ref[here, :] = level_in[here, :] - (volume_step * wet_ref[here, :]) * (
            east - pltpu.roll(east, 1, 1) + north - below
        )

    for start in range(0, tall, 8):
        fluxes(start)
        if start:
            levels(start)
    levels(0)
    fourier_sums(rows, level_ref, table_ref, out_ref)


def legendre_kernel(band, got_ref, legendre_ref, weight_ref, love_ref, out_ref, line_ref, back_ref):
    total, degrees = legendre_ref.shape
    bands = total // band
    line_ref[...] = jnp.zeros_like(line_ref)
    lane = lax.broadcasted_iota(jnp.int32, (8, MSG), 1)
    for index in range(bands):
        pair = got_ref[4 * index]
        for part in range(1, 4):
            pair = pair + got_ref[4 * index + part]
        piece = jnp.concatenate([pair, jnp.zeros((6, MSG), HIGH)], axis=0)
        piece = jnp.where(lane < band, piece, 0.0)
        tile, offset = divmod(band * index, LANES)
        if offset:
            piece = pltpu.roll(piece, offset, 1)
        where = slice(tile * LANES, tile * LANES + MSG)
        line_ref[:, where] = line_ref[:, where] + piece
    coeff = jnp.zeros((8, degrees), HIGH)
    for start in range(0, total, 256):
        where = slice(start, start + 256)
        weighted = (line_ref[:, where] * weight_ref[:, where]).astype(LOW)
        coeff = coeff + jnp.dot(weighted, legendre_ref[where, :], preferred_element_type=HIGH)
    scaled = (coeff * love_ref[...]).astype(LOW)
    back_ref[:, :LANES] = jnp.zeros((8, LANES), HIGH)
    back_ref[:, LANES + total :] = jnp.zeros((8, back_ref.shape[1] - LANES - total), HIGH)
    for start in range(0, total, 256):
        back_ref[:, LANES + start : LANES + start + 256] = lax.dot_general(
            scaled,
            legendre_ref[start : start + 256, :],
            (((1,), (1,)), ((), ())),
            preferred_element_type=HIGH,
        )
    for index in range(bands):
        tile, offset = divmod(band * index - HALO + LANES, LANES)
        piece = back_ref[:, tile * LANES : tile * LANES + 384]
        if offset:
            piece = pltpu.roll(piece, 384 - offset, 1)
        pair = piece[:2, :MSG]
        for part in range(4):
            out_ref[4 * index + part] = pair


def shifted(value, axis, by):
    count = lax.axis_size(axis)
    return lax.ppermute(value, axis, [(i, (i + by) % count) for i in range(count)])


def shifted_open(value, axis, by):
    count = lax.axis_size(axis)
    pairs = [(i, i + by) for i in range(count) if 0 <= i + by < count]
    return lax.ppermute(value, axis, pairs)


def with_ghosts(fields):
    rows = fields[0].shape[0]
    from_east = shifted(jnp.stack([f[:, :LANES] for f in fields]), "lon", -1)
    from_west = shifted(jnp.stack([f[:, -LANES:] for f in fields]), "lon", 1)
    lane = lax.broadcasted_iota(jnp.int32, from_east.shape, 2)
    tile = jnp.where(lane < HALO, from_east, jnp.where(lane >= LANES - HALO, from_west, 0.0))
    wide = [jnp.concatenate([f, tile[i]], axis=1) for i, f in enumerate(fields)]
    from_north = shifted_open(jnp.stack([f[:16] for f in wide]), "lat", -1)
    from_south = shifted_open(jnp.stack([f[rows - 16 :] for f in wide]), "lat", 1)
    return [
        jnp.concatenate([f, from_north[i, :HALO], from_south[i, 16 - HALO :]], axis=0)
        for i, f in enumerate(wide)
    ]


def shards(
    height,
    flux_east,
    flux_north,
    bathymetry,
    wet_mask,
    wavenumber,
    legendre,
    quadrature,
    love_factor,
):
    lon_count = lax.axis_size("lon")
    lat_count = lax.axis_size("lat")
    rows, cols = height.shape
    slots = wavenumber.shape[0]
    total_cols = cols * lon_count
    total_rows = rows * lat_count
    tall, wide = rows + 2 * HALO, cols + LANES
    devices = lat_count * lon_count
    padded_rows = -(-rows // 16) * 16

    lane = jnp.arange(wide, dtype=jnp.int32)
    offset = jnp.where(lane < cols + LANES // 2, lane, lane - wide)
    columns = (lax.axis_index("lon") * cols + offset + total_cols) % total_cols
    product = wavenumber[:, None] * columns[None, :] % total_cols
    angle = product.astype(HIGH) * (2.0 * math.pi / total_cols)
    basis = jnp.stack([jnp.cos(angle), -jnp.sin(angle)], axis=1).reshape(2 * slots, wide)
    basis_high = lax.reduce_precision(basis, 8, 7)
    basis_low = (basis - basis_high).astype(LOW)
    basis_high = basis_high.astype(LOW)
    synth = jnp.concatenate([basis_high, basis_low, basis_high, jnp.zeros_like(basis_low)], axis=0)
    table = jnp.concatenate([basis_high[:, :cols], basis_low[:, :cols]], axis=0).T

    wetness = wet_mask.astype(HIGH)
    level, east, north, bathy, wet = with_ghosts(
        [height, flux_east, flux_north, bathymetry, wetness]
    )
    row = lax.broadcasted_iota(jnp.int32, (tall, wide), 0)
    east_open = retain_factor * wet * jnp.roll(wet, -1, axis=1)
    north_open = retain_factor * wet * jnp.roll(wet, -1, axis=0)
    north_open = jnp.where(row == rows + HALO - 1, 0.0, north_open)
    weight = jnp.broadcast_to((quadrature / math.sqrt(total_cols))[None, :], (8, total_rows))
    love = jnp.broadcast_to(love_factor[None, :], (8, love_factor.shape[0]))
    legendre = legendre.reshape(legendre.shape[1:])

    field = jax.ShapeDtypeStruct((tall, wide), HIGH)
    message = jax.ShapeDtypeStruct((devices, 2, MSG), HIGH)
    small = pltpu.CompilerParams(vmem_limit_bytes=24 * 2**20)

    sums = pl.pallas_call(
        lambda *refs: first_kernel(padded_rows, *refs),
        out_shape=message,
        in_specs=[VMEM] * 2,
        out_specs=VMEM,
        compiler_params=small,
        name="first_sums",
    )(in_vmem(level), in_vmem(table))

    def advance(counter, carry):
        level, east, north, sums = carry
        spectral = lax.all_to_all(sums, BOTH, split_axis=0, concat_axis=0, tiled=True)
        back = pl.pallas_call(
            lambda *refs: legendre_kernel(rows, *refs),
            out_shape=message,
            in_specs=[VMEM] * 4,
            out_specs=VMEM,
            scratch_shapes=[
                pltpu.VMEM((8, total_rows + LANES), HIGH),
                pltpu.VMEM((8, total_rows + 4 * LANES), HIGH),
            ],
            compiler_params=small,
            name="legendre_pair",
        )(spectral, in_vmem(legendre), in_vmem(weight), in_vmem(love))
        bands = lax.all_to_all(back, BOTH, split_axis=0, concat_axis=0, tiled=True)
        return pl.pallas_call(
            lambda *refs: grid_kernel(padded_rows, *refs),
            out_shape=(field, field, field, message),
            in_specs=[VMEM] * 10,
            out_specs=(VMEM,) * 4,
            scratch_shapes=[
                pltpu.VMEM((2 * slots, MSG), HIGH),
                pltpu.VMEM((tall + 8, wide), HIGH),
                pltpu.VMEM((tall + 8, wide), HIGH),
            ],
            input_output_aliases={1: 0, 2: 1, 3: 2},
            compiler_params=small,
            name="grid_update",
        )(
            bands,
            in_vmem(level),
            in_vmem(east),
            in_vmem(north),
            in_vmem(bathy),
            in_vmem(wet),
            in_vmem(east_open),
            in_vmem(north_open),
            in_vmem(synth),
            in_vmem(table),
        )

    carry = (level, east, north, sums)
    for counter in range(STEPS):
        carry = advance(counter, carry)
    level, east, north, sums = carry
    return (level[:rows, :cols], east[:rows, :cols], north[:rows, :cols])


def solution(mesh):
    placed = (
        P("lat", "lon"),
        P("lat", "lon"),
        P("lat", "lon"),
        P("lat", "lon"),
        P("lat", "lon"),
        P(),
        P("lat", None, "lon"),
        P(),
        P("lon"),
    )
    return jax.shard_map(
        shards,
        mesh=mesh,
        in_specs=placed,
        out_specs=(P("lat", "lon"), P("lat", "lon"), P("lat", "lon")),
        check_vma=False,
    )
```

```python
import math

import jax
import jax.numpy as jnp
from jax import lax
from jax.experimental import pallas as pl
from jax.experimental.pallas import tpu as pltpu
from jax.sharding import PartitionSpec as P

STEPS = 12
HALO = STEPS
LANES = 128
SECOND = 192
MSG = 384
SLOT = 16

gravity_step = 0.12
volume_step = 0.12
retain_factor = 0.97

BOTH = ("lat", "lon")
VMEM = pl.BlockSpec(memory_space=pltpu.VMEM)
HIGH = jnp.float32
LOW = jnp.bfloat16


def in_vmem(value):
    return pltpu.with_memory_space_constraint(value, pltpu.VMEM)


def in_hbm(value):
    return pltpu.with_memory_space_constraint(value, pltpu.HBM)


def lanes_of(shape):
    return lax.broadcasted_iota(jnp.int32, shape, 1)


def rows_of(shape):
    return lax.broadcasted_iota(jnp.int32, shape, 0)


def split_pair(value):
    high = value.astype(LOW)
    return high, (value - high.astype(HIGH)).astype(LOW)


def received(got_ref, line_ref):
    every = got_ref.shape[0]
    count = every // 4
    tiles = []
    for tile in range(MSG // LANES):
        base = tile * every
        line_ref[base : base + every, :] = got_ref[:, tile * LANES : (tile + 1) * LANES]
        total = line_ref[pl.ds(base, count, stride=4), :]
        for part in range(1, 4):
            total = total + line_ref[pl.ds(base + part, count, stride=4), :]
        tiles.append(total)
    return jnp.concatenate(tiles, axis=1)


def send(message, out_ref, line_ref):
    every = out_ref.shape[0]
    for tile in range(MSG // LANES):
        base, block = tile * every, slice(tile * LANES, (tile + 1) * LANES)
        for part in range(4):
            line_ref[pl.ds(base + part, every // 4, stride=4), :] = message[:, block]
        out_ref[:, block] = line_ref[base : base + every, :]


def second_part(message):
    return pltpu.roll(message[:, LANES:], 2 * LANES - (SECOND - LANES), 1)


def fourier_sums(rows, read, table_ref, out_ref, line_ref):
    cols = table_ref.shape[0]
    total = jnp.zeros((2 * rows, LANES), HIGH)
    for start in range(0, cols, 256):
        high, low = split_pair(read(start))
        both = jnp.concatenate([high, low], axis=0)
        total = total + jnp.dot(both, table_ref[start : start + 256, :], preferred_element_type=HIGH)
    half = total[:rows] + total[rows:]
    half = half + pltpu.roll(half, LANES // 2, 1)
    half = jnp.concatenate([half, jnp.zeros((256 - rows, LANES), HIGH)], axis=0)
    sums = jnp.transpose(half)
    slots = out_ref.shape[0] // 4
    first = sums[:slots]
    second = pltpu.roll(sums[slots : 2 * slots], SECOND - LANES, 1)
    middle = jnp.where(lanes_of((slots, LANES)) < SECOND - LANES, first[:, LANES:], second[:, :LANES])
    send(jnp.concatenate([first[:, :LANES], middle, second[:, LANES:]], axis=1), out_ref, line_ref)


def first_kernel(rows, height_ref, basis_ref, out_ref, table_ref, synth_ref, line_ref):
    own, cols = height_ref.shape
    basis = basis_ref[...]
    high, low = split_pair(basis)
    count = basis.shape[0]
    synth_ref[:count, :] = high
    synth_ref[count : 2 * count, :] = low
    synth_ref[2 * count : 3 * count, :] = high
    synth_ref[3 * count :, :] = jnp.zeros_like(high)
    for start in range(0, cols, LANES):
        block = slice(start, start + LANES)
        both = jnp.concatenate([high[:, block].astype(HIGH), low[:, block].astype(HIGH)], axis=0)
        table_ref[block, :] = jnp.transpose(both).astype(LOW)

    def read(start):
        block = height_ref[:, start : start + 256]
        return jnp.concatenate([block, jnp.zeros((rows - own, 256), HIGH)], axis=0)

    fourier_sums(rows, read, table_ref, out_ref, line_ref)


def above_of(ref, start, tall):
    if start + 8 < tall:
        return ref[start + 1 : start + 9, :]
    return jnp.concatenate([ref[start + 1 : tall, :], ref[:1, :]], axis=0)


def grid_kernel(rows, last, *refs):
    (got_ref, level_in, east_in, north_in, bathy_ref, wet_ref, east_open_ref, north_open_ref) = refs[:8]
    synth_ref, refs = refs[8], refs[9:]
    if last:
        level_ref, east_ref, north_ref, pot_ref, depth_ref, south_ref, line_ref = refs
    else:
        table_ref, level_ref, east_ref, north_ref, out_ref = refs[:5]
        pot_ref, depth_ref, south_ref, line_ref = refs[5:]
    tall, wide = level_in.shape
    own, cols = level_ref.shape
    message = received(got_ref, line_ref)
    slots = message.shape[0]
    back = jnp.concatenate([message[:, : 2 * LANES], second_part(message)], axis=0)
    back = back * (1.0 / math.sqrt(4 * (wide - LANES)))
    back = jnp.where(
        lanes_of(back.shape) < tall - HALO,
        pltpu.roll(back, 2 * LANES - HALO, 1),
        pltpu.roll(back, tall - HALO, 1),
    )
    high, low = split_pair(back)
    high, low = high.astype(HIGH), low.astype(HIGH)
    stacked = jnp.concatenate([high, high, low, jnp.zeros_like(low)], axis=0)
    factors = jnp.transpose(stacked)[:tall].astype(LOW)
    half_gravity = gravity_step * 0.5
    for start in range(0, wide, 256):
        block = slice(start, min(start + 256, wide))
        pull = jnp.dot(factors, synth_ref[:, block], preferred_element_type=HIGH)
        level = level_in[:, block]
        pot_ref[:tall, block] = level + pull
        depth_ref[:tall, block] = (half_gravity * wet_ref[:, block]) * jnp.maximum(
            bathy_ref[:, block] + level, 0.0
        )
    pot_ref[tall:, :] = pot_ref[:8, :]
    depth_ref[tall:, :] = depth_ref[:8, :]

    def update(start):
        here = slice(start, start + 8)
        above = slice(start + 1, start + 9)
        pot, depth = pot_ref[here, :], depth_ref[here, :]
        pot_east, depth_east = pltpu.roll(pot, wide - 1, 1), pltpu.roll(depth, wide - 1, 1)
        east = east_open_ref[here, :] * (
            east_in[here, :] - (depth + depth_east) * (pot_east - pot)
        )
        north = north_open_ref[here, :] * (
            north_in[here, :] - (depth + depth_ref[above, :]) * (pot_ref[above, :] - pot)
        )
        south_ref[start + 8 : start + 16, :] = north
        below = south_ref[start + 7 : start + 15, :]
        level = level_in[here, :] - (volume_step * wet_ref[here, :]) * (
            east - pltpu.roll(east, 1, 1) + north - below
        )
        if start < own:
            east_ref[here, :] = east[:, :cols]
            north_ref[here, :] = north[:, :cols]
            level_ref[here, :] = level[:, :cols]

    if last:
        update(tall - 8)
        south_ref[:8, :] = south_ref[tall : tall + 8, :]
        for start in range(0, own, 8):
            update(start)
    else:
        seam = tall - 2 * HALO
        south_ref[seam : seam + 8, :] = jnp.zeros((8, wide), HIGH)
        for start in range(seam, tall, 8):
            update(start)
        south_ref[:8, :] = south_ref[tall : tall + 8, :]
        for start in range(0, seam, 8):
            update(start)
        fix = slice(seam, seam + 8)
        row = rows_of((8, wide))
        missed = jnp.where(row == 0, south_ref[seam + 7 : seam + 15, :], 0.0)
        level_ref[fix, :] = level_ref[fix, :] + (volume_step * wet_ref[fix, :]) * missed
        def read(start):
            return level_ref[:rows, start : start + 256]

        fourier_sums(rows, read, table_ref, out_ref, line_ref)


def legendre_kernel(band, first, got_ref, legendre_ref, weight_ref, love_ref, *refs):
    if first:
        out_ref, held_ref, tiles_ref, line_ref, copies = refs
    else:
        out_ref, tiles_ref, line_ref = refs
        held_ref = legendre_ref
    total, degrees = legendre_ref.shape
    bands = total // band
    count = total // LANES
    chunk = 2 * LANES
    step = band - LANES

    def copy(start):
        block = pl.ds(start, chunk)
        return pltpu.make_async_copy(
            legendre_ref.at[block, :], held_ref.at[block, :], copies.at[start // chunk]
        )

    if first:
        for start in range(0, total, chunk):
            copy(start).start()

    message = received(got_ref, line_ref)
    tall = tiles_ref.shape[0] // 2
    for k, part in enumerate((message[:, :chunk], second_part(message))):
        part = jnp.where(lanes_of(part.shape) < band, part, 0.0)
        part = pltpu.roll(part, 0, 1, stride=step, stride_axis=0)
        early, late = part[:, :LANES], part[:, LANES:]
        zeros = jnp.zeros((tall - bands, LANES), HIGH)
        row = rows_of((tall, LANES))
        early = jnp.concatenate([early, zeros], axis=0)
        late = jnp.concatenate([late, zeros], axis=0)
        wraps = LANES // step
        line = (
            pltpu.roll(late, 1, 0)
            + jnp.where(row < wraps, early, 0.0)
            + jnp.where(row >= wraps + 2, pltpu.roll(early, 2, 0), 0.0)
        )
        tiles_ref[k * tall : (k + 1) * tall, :] = line * weight_ref[...]
    coeff = jnp.zeros((2, degrees), HIGH)
    for start in range(0, total, chunk):
        tile = start // LANES
        weighted = jnp.concatenate(
            [tiles_ref[pl.ds(tile + i, 2, stride=tall), :] for i in range(2)], axis=1
        ).astype(LOW)
        if first:
            copy(start).wait()
        coeff = coeff + jnp.dot(
            weighted, held_ref[start : start + chunk, :], preferred_element_type=HIGH
        )
    scaled = (coeff * love_ref[...]).astype(LOW)
    tiles_ref[...] = jnp.zeros_like(tiles_ref)
    for start in range(0, total, chunk):
        back = lax.dot_general(
            scaled,
            held_ref[start : start + chunk, :],
            (((1,), (1,)), ((), ())),
            preferred_element_type=HIGH,
        )
        row = tall - 2 - start // LANES
        for i in range(2):
            tiles_ref[pl.ds(row - i, 2, stride=tall), :] = back[:, i * LANES : (i + 1) * LANES]
    parts = []
    reach = LANES - HALO + step * (bands - 1 - rows_of((bands, LANES)))
    for k in range(2):

        def tile(shift):
            begin = (k + 1) * tall - bands - shift
            return tiles_ref[begin : begin + bands, :]

        window = jnp.concatenate(
            [
                jnp.where(reach < LANES, tile(0), tile(3)),
                jnp.where(reach < 2 * LANES, tile(1), tile(4)),
                tile(2),
            ],
            axis=1,
        )
        shift = (k * SECOND - LANES + HALO - step * (bands - 1)) % MSG
        window = pltpu.roll(window, shift, 1)
        parts.append(pltpu.roll(window, 0, 1, stride=step, stride_axis=0))
    result = jnp.where(lanes_of(parts[0].shape) < SECOND, parts[0], parts[1])
    for index in range(bands):
        at = bands - 1 - index
        out_ref[4 * index : 4 * index + 4, :] = jnp.broadcast_to(result[at : at + 1, :], (4, MSG))


def ghost_tile(index, east, west):
    lane = lanes_of(east.shape)
    east = pltpu.roll(east, LANES - SLOT * index, 1) if index else east
    west = pltpu.roll(west, LANES - SLOT * (index + 1), 1)
    return jnp.where(lane < HALO, east, jnp.where(lane >= LANES - HALO, west, 0.0))


def column_edge_kernel(*refs):
    fields, (west_ref, east_ref) = refs[:-2], refs[-2:]
    lane = lanes_of(west_ref.shape)
    west = jnp.zeros(west_ref.shape, HIGH)
    east = jnp.zeros(east_ref.shape, HIGH)
    for index in range(len(fields) // 2):
        left, right = (ref[...].astype(HIGH) for ref in fields[2 * index : 2 * index + 2])
        here = (lane >= SLOT * index) & (lane < SLOT * (index + 1))
        west = jnp.where(here, pltpu.roll(left, SLOT * index, 1) if index else left, west)
        east = jnp.where(here, pltpu.roll(right, SLOT * (index + 1), 1), east)
    west_ref[...] = west
    east_ref[...] = east


def row_edge_kernel(begin, *refs):
    fields, (from_east, from_west, unused_ref, out_ref) = refs[:-4], refs[-4:]
    cols = fields[0].shape[1]
    keep = slice(begin, begin + HALO)
    out_ref[len(fields) // 2 * HALO :, :] = jnp.zeros_like(out_ref[len(fields) // 2 * HALO :, :])
    for index in range(len(fields) // 2):
        both = jnp.concatenate([ref[...].astype(HIGH) for ref in fields[2 * index : 2 * index + 2]], axis=0)
        where = slice(HALO * index, HALO * (index + 1))
        out_ref[where, :cols] = both[keep]
        out_ref[where, cols:] = ghost_tile(index, from_east[...], from_west[...])[keep]


def assemble_kernel(*refs):
    fields, refs = refs[:5], refs[5:]
    (from_east, from_west, from_north, from_south), refs = refs[:4], refs[4:]
    outs, (east_open_ref, north_open_ref, mask_ref, copies) = refs[:5], refs[5:]
    rows, cols = fields[0].shape
    tall, wide = outs[0].shape
    targets = [out.at[:rows, :cols] for out in outs[:4]] + [mask_ref]
    moves = [
        pltpu.make_async_copy(field, target, copies.at[index])
        for index, (field, target) in enumerate(zip(fields, targets))
    ]
    for move in moves[::-1]:
        move.start()
    for index, out in enumerate(outs):
        out[:rows, cols:] = ghost_tile(index, from_east[...], from_west[...])
        begin = HALO * index
        out[rows:, :] = jnp.concatenate(
            [from_north[begin : begin + HALO, :], from_south[begin : begin + HALO, :]], axis=0
        )
    moves[4].wait()
    wet_ref = outs[4]
    wet_ref[:rows, :cols] = mask_ref[...].astype(HIGH)
    for start in range(0, tall, 8):
        here = slice(start, start + 8)
        wet = wet_ref[here, :]
        above = above_of(wet_ref, start, tall)
        if start <= rows + HALO - 1 < start + 8:
            above = jnp.where(rows_of(above.shape) == rows + HALO - 1 - start, 0.0, above)
        east_open_ref[here, :] = retain_factor * wet * pltpu.roll(wet, wide - 1, 1)
        north_open_ref[here, :] = retain_factor * wet * above
    for move in moves[:4]:
        move.wait()


def shifted(value, axis, by):
    count = lax.axis_size(axis)
    return lax.ppermute(value, axis, [(i, (i + by) % count) for i in range(count)])


def shifted_open(value, axis, by):
    count = lax.axis_size(axis)
    pairs = [(i, i + by) for i in range(count) if 0 <= i + by < count]
    return lax.ppermute(value, axis, pairs)


def shards(
    height,
    flux_east,
    flux_north,
    bathymetry,
    wet_mask,
    wavenumber,
    legendre,
    quadrature,
    love_factor,
):
    lon_count = lax.axis_size("lon")
    lat_count = lax.axis_size("lat")
    rows, cols = height.shape
    slots = wavenumber.shape[0]
    total_cols = cols * lon_count
    total_rows = rows * lat_count
    tall, wide = rows + 2 * HALO, cols + LANES
    devices = lat_count * lon_count
    padded_rows = -(-rows // 16) * 16
    legendre = legendre.reshape(legendre.shape[1:])
    degrees = legendre.shape[1]
    small = pltpu.CompilerParams(vmem_limit_bytes=12 * 2**20)
    message = jax.ShapeDtypeStruct((devices, MSG), HIGH)
    field = jax.ShapeDtypeStruct((tall, wide), HIGH)
    line = pltpu.VMEM((MSG // LANES * devices, LANES), HIGH)
    fields = [height, flux_east, flux_north, bathymetry, wet_mask]

    column_edge = jax.ShapeDtypeStruct((rows, LANES), HIGH)
    edge_spec = pl.BlockSpec((rows, LANES), lambda i: (0, 0))
    west_edge, east_edge = pl.pallas_call(
        column_edge_kernel,
        grid=(1,),
        out_shape=(column_edge,) * 2,
        in_specs=[edge_spec, pl.BlockSpec((rows, LANES), lambda i: (0, cols // LANES - 1))] * 5,
        out_specs=(edge_spec,) * 2,
        compiler_params=small,
        name="column_edges",
    )(*[in_hbm(f) for f in fields for _ in range(2)])
    from_east = shifted(west_edge, "lon", -1)
    from_west = shifted(east_edge, "lon", 1)

    def row_edge(start, keep, after):
        block = [pl.BlockSpec((8, cols), lambda i, at=start // 8 + n: (at, 0)) for n in range(2)]
        ghost = pl.BlockSpec((16, LANES), lambda i: (0, 0))
        return pl.pallas_call(
            lambda *refs: row_edge_kernel(keep, *refs),
            grid=(1,),
            out_shape=jax.ShapeDtypeStruct((64, wide), HIGH),
            in_specs=block * 5 + [ghost, ghost, pl.BlockSpec(memory_space=pl.ANY)],
            out_specs=pl.BlockSpec((64, wide), lambda i: (0, 0)),
            compiler_params=small,
            name="row_edges",
        )(
            *[in_hbm(f) for f in fields for _ in range(2)],
            from_east[start : start + 16],
            from_west[start : start + 16],
            after,
        )

    lane = jnp.arange(wide, dtype=jnp.int32)
    offset = jnp.where(lane < cols + LANES // 2, lane, lane - wide)
    columns = (lax.axis_index("lon") * cols + offset + total_cols) % total_cols
    product = wavenumber[:, None] * columns[None, :] % total_cols
    angle = product.astype(HIGH) * (2.0 * math.pi / total_cols)
    basis = jnp.concatenate([jnp.cos(angle), -jnp.sin(angle)], axis=0)
    weight = (quadrature / math.sqrt(total_cols)).reshape(total_rows // LANES, LANES)
    weight = jnp.pad(weight, ((0, 40 - total_rows // LANES), (0, 0)))
    love = love_factor[None, :]

    sums, table, synth = pl.pallas_call(
        lambda *refs: first_kernel(padded_rows, *refs),
        out_shape=(
            message,
            pltpu.VMEM((cols, LANES), LOW),
            pltpu.VMEM((8 * slots, wide), LOW),
        ),
        in_specs=[VMEM] * 2,
        out_specs=(VMEM,) * 3,
        scratch_shapes=[line],
        compiler_params=small,
        name="first_sums",
    )(height, basis)

    held = pltpu.VMEM((tall, wide), HIGH)
    tiles = pltpu.VMEM((80, LANES), HIGH)
    for step in range(STEPS):
        first, last = step == 0, step == STEPS - 1
        spectral = lax.all_to_all(sums, BOTH, split_axis=0, concat_axis=0, tiled=True)
        if first:
            back, legendre = pl.pallas_call(
                lambda *refs: legendre_kernel(rows, True, *refs),
                out_shape=(message, pltpu.VMEM(legendre.shape, LOW)),
                in_specs=[VMEM, pl.BlockSpec(memory_space=pl.ANY), VMEM, VMEM],
                out_specs=(VMEM,) * 2,
                scratch_shapes=[tiles, line, pltpu.SemaphoreType.DMA((total_rows // 256,))],
                compiler_params=small,
                name="legendre_first",
            )(spectral, in_hbm(legendre), weight, love)
        else:
            back = pl.pallas_call(
                lambda *refs: legendre_kernel(rows, False, *refs),
                out_shape=message,
                in_specs=[VMEM] * 4,
                out_specs=VMEM,
                scratch_shapes=[tiles, line],
                compiler_params=small,
                name="legendre_pair",
            )(spectral, in_vmem(legendre), in_vmem(weight), in_vmem(love))
        if first:
            from_north = shifted_open(row_edge(0, 0, spectral), "lat", -1)
            from_south = shifted_open(row_edge(rows - 16, 16 - HALO, back), "lat", 1)
            level, east, north, bathy, wet, east_open, north_open = pl.pallas_call(
                assemble_kernel,
                out_shape=(held,) * 7,
                in_specs=[pl.BlockSpec(memory_space=pl.ANY)] * 5 + [VMEM] * 4,
                out_specs=(VMEM,) * 7,
                scratch_shapes=[pltpu.VMEM((rows, cols), jnp.int32), pltpu.SemaphoreType.DMA((5,))],
                compiler_params=small,
                name="assemble",
            )(*[in_hbm(f) for f in fields], from_east, from_west, from_north, from_south)
        bands = lax.all_to_all(back, BOTH, split_axis=0, concat_axis=0, tiled=True)
        operands = [bands] + [
            in_vmem(x) for x in (level, east, north, bathy, wet, east_open, north_open, synth, table)
        ]
        scratch = [pltpu.VMEM((tall + 8, wide), HIGH)] * 3 + [line]
        if last:
            own = jax.ShapeDtypeStruct((rows, cols), HIGH)
            return pl.pallas_call(
                lambda *refs: grid_kernel(padded_rows, True, *refs),
                out_shape=(own,) * 3,
                in_specs=[VMEM] * 9,
                out_specs=(VMEM,) * 3,
                scratch_shapes=scratch,
                compiler_params=small,
                name="grid_last",
            )(*operands[:9])
        level, east, north, sums = pl.pallas_call(
            lambda *refs: grid_kernel(padded_rows, False, *refs),
            out_shape=(field, field, field, message),
            in_specs=[VMEM] * 10,
            out_specs=(VMEM,) * 4,
            scratch_shapes=scratch,
            input_output_aliases={1: 0, 2: 1, 3: 2},
            compiler_params=small,
            name="grid_update",
        )(*operands)


def solution(mesh):
    placed = (
        P("lat", "lon"),
        P("lat", "lon"),
        P("lat", "lon"),
        P("lat", "lon"),
        P("lat", "lon"),
        P(),
        P("lat", None, "lon"),
        P(),
        P("lon"),
    )
    return jax.shard_map(
        shards,
        mesh=mesh,
        in_specs=placed,
        out_specs=(P("lat", "lon"), P("lat", "lon"), P("lat", "lon")),
        check_vma=False,
    )
```

```python
import math

import jax
import jax.numpy as jnp
from jax import lax
from jax.experimental import pallas as pl
from jax.experimental.pallas import tpu as pltpu
from jax.sharding import PartitionSpec as P

STEPS = 12
HALO = STEPS
LANES = 128
SECOND = 192
MSG = 384
SLOT = 16

gravity_step = 0.12
volume_step = 0.12
retain_factor = 0.97

BOTH = ("lat", "lon")
VMEM = pl.BlockSpec(memory_space=pltpu.VMEM)
HIGH = jnp.float32
LOW = jnp.bfloat16


def in_vmem(value):
    return pltpu.with_memory_space_constraint(value, pltpu.VMEM)


def in_hbm(value):
    return pltpu.with_memory_space_constraint(value, pltpu.HBM)


def lanes_of(shape):
    return lax.broadcasted_iota(jnp.int32, shape, 1)


def rows_of(shape):
    return lax.broadcasted_iota(jnp.int32, shape, 0)


def split_pair(value):
    high = value.astype(LOW)
    return high, (value - high.astype(HIGH)).astype(LOW)


def received(got_ref, line_ref):
    every = got_ref.shape[0]
    count = every // 4
    tiles = []
    for tile in range(MSG // LANES):
        base = tile * every
        line_ref[base : base + every, :] = got_ref[:, tile * LANES : (tile + 1) * LANES]
        total = line_ref[pl.ds(base, count, stride=4), :]
        for part in range(1, 4):
            total = total + line_ref[pl.ds(base + part, count, stride=4), :]
        tiles.append(total)
    return jnp.concatenate(tiles, axis=1)


def send(message, out_ref, line_ref):
    every = out_ref.shape[0]
    for tile in range(MSG // LANES):
        base, block = tile * every, slice(tile * LANES, (tile + 1) * LANES)
        for part in range(4):
            line_ref[pl.ds(base + part, every // 4, stride=4), :] = message[:, block]
        out_ref[:, block] = line_ref[base : base + every, :]


def second_part(message):
    return pltpu.roll(message[:, LANES:], 2 * LANES - (SECOND - LANES), 1)


def fourier_sums(rows, read, table_ref, out_ref, line_ref):
    cols = table_ref.shape[0]
    total = jnp.zeros((2 * rows, LANES), HIGH)
    for start in range(0, cols, 256):
        high, low = split_pair(read(start))
        both = jnp.concatenate([high, low], axis=0)
        total = total + jnp.dot(both, table_ref[start : start + 256, :], preferred_element_type=HIGH)
    half = total[:rows] + total[rows:]
    half = half + pltpu.roll(half, LANES // 2, 1)
    half = jnp.concatenate([half, jnp.zeros((256 - rows, LANES), HIGH)], axis=0)
    sums = jnp.transpose(half)
    slots = out_ref.shape[0] // 4
    first = sums[:slots]
    second = pltpu.roll(sums[slots : 2 * slots], SECOND - LANES, 1)
    middle = jnp.where(lanes_of((slots, LANES)) < SECOND - LANES, first[:, LANES:], second[:, :LANES])
    send(jnp.concatenate([first[:, :LANES], middle, second[:, LANES:]], axis=1), out_ref, line_ref)


def first_kernel(rows, height_ref, basis_ref, out_ref, table_ref, synth_ref, line_ref):
    own, cols = height_ref.shape
    basis = basis_ref[...]
    high, low = split_pair(basis)
    count = basis.shape[0]
    synth_ref[:count, :] = high
    synth_ref[count : 2 * count, :] = low
    synth_ref[2 * count : 3 * count, :] = high
    synth_ref[3 * count :, :] = jnp.zeros_like(high)
    for start in range(0, cols, LANES):
        block = slice(start, start + LANES)
        both = jnp.concatenate([high[:, block].astype(HIGH), low[:, block].astype(HIGH)], axis=0)
        table_ref[block, :] = jnp.transpose(both).astype(LOW)

    def read(start):
        block = height_ref[:, start : start + 256]
        return jnp.concatenate([block, jnp.zeros((rows - own, 256), HIGH)], axis=0)

    fourier_sums(rows, read, table_ref, out_ref, line_ref)


def above_of(ref, start, tall):
    if start + 8 < tall:
        return ref[start + 1 : start + 9, :]
    return jnp.concatenate([ref[start + 1 : tall, :], ref[:1, :]], axis=0)


def grid_kernel(rows, last, *refs):
    (got_ref, level_in, east_in, north_in, bathy_ref, wet_ref, east_open_ref, north_open_ref) = refs[:8]
    synth_ref, refs = refs[8], refs[9:]
    if last:
        level_ref, east_ref, north_ref, pot_ref, depth_ref, south_ref, line_ref = refs
    else:
        table_ref, level_ref, east_ref, north_ref, out_ref = refs[:5]
        pot_ref, depth_ref, south_ref, line_ref = refs[5:]
    tall, wide = level_in.shape
    own, cols = level_ref.shape
    message = received(got_ref, line_ref)
    slots = message.shape[0]
    back = jnp.concatenate([message[:, : 2 * LANES], second_part(message)], axis=0)
    back = back * (1.0 / math.sqrt(4 * (wide - LANES)))
    back = jnp.where(
        lanes_of(back.shape) < tall - HALO,
        pltpu.roll(back, 2 * LANES - HALO, 1),
        pltpu.roll(back, tall - HALO, 1),
    )
    high, low = split_pair(back)
    high, low = high.astype(HIGH), low.astype(HIGH)
    stacked = jnp.concatenate([high, high, low, jnp.zeros_like(low)], axis=0)
    factors = jnp.transpose(stacked)[:tall].astype(LOW)
    half_gravity = gravity_step * 0.5
    for start in range(0, wide, 256):
        block = slice(start, min(start + 256, wide))
        pull = jnp.dot(factors, synth_ref[:, block], preferred_element_type=HIGH)
        level = level_in[:, block]
        pot_ref[:tall, block] = level + pull
        depth_ref[:tall, block] = (half_gravity * wet_ref[:, block]) * jnp.maximum(
            bathy_ref[:, block] + level, 0.0
        )
    pot_ref[tall:, :] = pot_ref[:8, :]
    depth_ref[tall:, :] = depth_ref[:8, :]

    def update(start):
        here = slice(start, start + 8)
        above = slice(start + 1, start + 9)
        pot, depth = pot_ref[here, :], depth_ref[here, :]
        pot_east, depth_east = pltpu.roll(pot, wide - 1, 1), pltpu.roll(depth, wide - 1, 1)
        east = east_open_ref[here, :] * (
            east_in[here, :] - (depth + depth_east) * (pot_east - pot)
        )
        north = north_open_ref[here, :] * (
            north_in[here, :] - (depth + depth_ref[above, :]) * (pot_ref[above, :] - pot)
        )
        south_ref[start + 8 : start + 16, :] = north
        below = south_ref[start + 7 : start + 15, :]
        level = level_in[here, :] - (volume_step * wet_ref[here, :]) * (
            east - pltpu.roll(east, 1, 1) + north - below
        )
        if start < own:
            east_ref[here, :] = east[:, :cols]
            north_ref[here, :] = north[:, :cols]
            level_ref[here, :] = level[:, :cols]

    if last:
        update(tall - 8)
        south_ref[:8, :] = south_ref[tall : tall + 8, :]
        for start in range(0, own, 8):
            update(start)
    else:
        seam = tall - 2 * HALO
        south_ref[seam : seam + 8, :] = jnp.zeros((8, wide), HIGH)
        for start in range(seam, tall, 8):
            update(start)
        south_ref[:8, :] = south_ref[tall : tall + 8, :]
        for start in range(0, seam, 8):
            update(start)
        fix = slice(seam, seam + 8)
        row = rows_of((8, wide))
        missed = jnp.where(row == 0, south_ref[seam + 7 : seam + 15, :], 0.0)
        level_ref[fix, :] = level_ref[fix, :] + (volume_step * wet_ref[fix, :]) * missed
        def read(start):
            return level_ref[:rows, start : start + 256]

        fourier_sums(rows, read, table_ref, out_ref, line_ref)


def table_kernel(legendre_ref, unused_ref, held_ref, turned_ref, copies):
    total, degrees = legendre_ref.shape
    chunk = 2 * LANES
    ahead = 4

    def copy(start):
        block = pl.ds(start, chunk)
        return pltpu.make_async_copy(
            legendre_ref.at[block, :], held_ref.at[block, :], copies.at[start // chunk]
        )

    for start in range(0, ahead * chunk, chunk):
        copy(start).start()
    for start in range(0, total, chunk):
        copy(start).wait()
        if start + ahead * chunk < total:
            copy(start + ahead * chunk).start()
        turned_ref[:, start : start + chunk] = jnp.transpose(held_ref[start : start + chunk, :])


def legendre_kernel(
    band, got_ref, legendre_ref, weight_ref, love_ref, turned_ref, out_ref, tiles_ref, line_ref
):
    total, degrees = legendre_ref.shape
    bands = total // band
    chunk = 2 * LANES
    step = band - LANES

    message = received(got_ref, line_ref)
    tall = tiles_ref.shape[0] // 2
    for k, part in enumerate((message[:, :chunk], second_part(message))):
        part = jnp.where(lanes_of(part.shape) < band, part, 0.0)
        part = pltpu.roll(part, 0, 1, stride=step, stride_axis=0)
        early, late = part[:, :LANES], part[:, LANES:]
        zeros = jnp.zeros((tall - bands, LANES), HIGH)
        row = rows_of((tall, LANES))
        early = jnp.concatenate([early, zeros], axis=0)
        late = jnp.concatenate([late, zeros], axis=0)
        wraps = LANES // step
        line = (
            pltpu.roll(late, 1, 0)
            + jnp.where(row < wraps, early, 0.0)
            + jnp.where(row >= wraps + 2, pltpu.roll(early, 2, 0), 0.0)
        )
        tiles_ref[k * tall : (k + 1) * tall, :] = line * weight_ref[...]
    coeff = jnp.zeros((2, degrees), HIGH)
    for start in range(0, total, chunk):
        tile = start // LANES
        weighted = jnp.concatenate(
            [tiles_ref[pl.ds(tile + i, 2, stride=tall), :] for i in range(2)], axis=1
        ).astype(LOW)
        coeff = coeff + jnp.dot(
            weighted, legendre_ref[start : start + chunk, :], preferred_element_type=HIGH
        )
    coeff = jnp.concatenate([coeff * love_ref[...], jnp.zeros((6, degrees), HIGH)], axis=0)
    scaled = coeff.astype(LOW)
    tiles_ref[...] = jnp.zeros_like(tiles_ref)
    for start in range(0, total, chunk):
        back = jnp.dot(
            scaled, turned_ref[:, start : start + chunk], preferred_element_type=HIGH
        )
        row = tall - 2 - start // LANES
        for i in range(2):
            for k in range(2):
                at = k * tall + row - i
                tiles_ref[at : at + 1, :] = back[k : k + 1, i * LANES : (i + 1) * LANES]
    parts = []
    reach = LANES - HALO + step * (bands - 1 - rows_of((bands, LANES)))
    for k in range(2):

        def tile(shift):
            begin = (k + 1) * tall - bands - shift
            return tiles_ref[begin : begin + bands, :]

        window = jnp.concatenate(
            [
                jnp.where(reach < LANES, tile(0), tile(3)),
                jnp.where(reach < 2 * LANES, tile(1), tile(4)),
                tile(2),
            ],
            axis=1,
        )
        shift = (k * SECOND - LANES + HALO - step * (bands - 1)) % MSG
        window = pltpu.roll(window, shift, 1)
        parts.append(pltpu.roll(window, 0, 1, stride=step, stride_axis=0))
    result = jnp.where(lanes_of(parts[0].shape) < SECOND, parts[0], parts[1])
    for index in range(bands):
        at = bands - 1 - index
        out_ref[4 * index : 4 * index + 4, :] = jnp.broadcast_to(result[at : at + 1, :], (4, MSG))


def ghost_tile(index, east, west):
    lane = lanes_of(east.shape)
    east = pltpu.roll(east, LANES - SLOT * index, 1) if index else east
    west = pltpu.roll(west, LANES - SLOT * (index + 1), 1)
    return jnp.where(lane < HALO, east, jnp.where(lane >= LANES - HALO, west, 0.0))


def column_edge_kernel(*refs):
    fields, (west_ref, east_ref) = refs[:-2], refs[-2:]
    lane = lanes_of(west_ref.shape)
    west = jnp.zeros(west_ref.shape, HIGH)
    east = jnp.zeros(east_ref.shape, HIGH)
    for index in range(len(fields) // 2):
        left, right = (ref[...].astype(HIGH) for ref in fields[2 * index : 2 * index + 2])
        here = (lane >= SLOT * index) & (lane < SLOT * (index + 1))
        west = jnp.where(here, pltpu.roll(left, SLOT * index, 1) if index else left, west)
        east = jnp.where(here, pltpu.roll(right, SLOT * (index + 1), 1), east)
    west_ref[...] = west
    east_ref[...] = east


def row_edge_kernel(begin, *refs):
    fields, (from_east, from_west, unused_ref, out_ref) = refs[:-4], refs[-4:]
    cols = fields[0].shape[1]
    keep = slice(begin, begin + HALO)
    out_ref[len(fields) // 2 * HALO :, :] = jnp.zeros_like(out_ref[len(fields) // 2 * HALO :, :])
    for index in range(len(fields) // 2):
        both = jnp.concatenate([ref[...].astype(HIGH) for ref in fields[2 * index : 2 * index + 2]], axis=0)
        where = slice(HALO * index, HALO * (index + 1))
        out_ref[where, :cols] = both[keep]
        out_ref[where, cols:] = ghost_tile(index, from_east[...], from_west[...])[keep]


def assemble_kernel(*refs):
    fields, refs = refs[:5], refs[5:]
    (from_east, from_west, from_north, from_south), refs = refs[:4], refs[4:]
    outs, (east_open_ref, north_open_ref, mask_ref, copies) = refs[:5], refs[5:]
    rows, cols = fields[0].shape
    tall, wide = outs[0].shape
    targets = [out.at[:rows, :cols] for out in outs[:4]] + [mask_ref]
    moves = [
        pltpu.make_async_copy(field, target, copies.at[index])
        for index, (field, target) in enumerate(zip(fields, targets))
    ]
    for move in moves[4:] + moves[:4]:
        move.start()
    for index, out in enumerate(outs):
        out[:rows, cols:] = ghost_tile(index, from_east[...], from_west[...])
        begin = HALO * index
        out[rows:, :] = jnp.concatenate(
            [from_north[begin : begin + HALO, :], from_south[begin : begin + HALO, :]], axis=0
        )
    moves[4].wait()
    wet_ref = outs[4]
    wet_ref[:rows, :cols] = mask_ref[...].astype(HIGH)
    for start in range(0, tall, 8):
        here = slice(start, start + 8)
        wet = wet_ref[here, :]
        above = above_of(wet_ref, start, tall)
        if start <= rows + HALO - 1 < start + 8:
            above = jnp.where(rows_of(above.shape) == rows + HALO - 1 - start, 0.0, above)
        east_open_ref[here, :] = retain_factor * wet * pltpu.roll(wet, wide - 1, 1)
        north_open_ref[here, :] = retain_factor * wet * above
    for move in moves[:4]:
        move.wait()


def shifted(value, axis, by):
    count = lax.axis_size(axis)
    return lax.ppermute(value, axis, [(i, (i + by) % count) for i in range(count)])


def shifted_open(value, axis, by):
    count = lax.axis_size(axis)
    pairs = [(i, i + by) for i in range(count) if 0 <= i + by < count]
    return lax.ppermute(value, axis, pairs)


def shards(
    height,
    flux_east,
    flux_north,
    bathymetry,
    wet_mask,
    wavenumber,
    legendre,
    quadrature,
    love_factor,
):
    lon_count = lax.axis_size("lon")
    lat_count = lax.axis_size("lat")
    rows, cols = height.shape
    slots = wavenumber.shape[0]
    total_cols = cols * lon_count
    total_rows = rows * lat_count
    tall, wide = rows + 2 * HALO, cols + LANES
    devices = lat_count * lon_count
    padded_rows = -(-rows // 16) * 16
    legendre = legendre.reshape(legendre.shape[1:])
    degrees = legendre.shape[1]
    small = pltpu.CompilerParams(vmem_limit_bytes=12 * 2**20)
    message = jax.ShapeDtypeStruct((devices, MSG), HIGH)
    field = jax.ShapeDtypeStruct((tall, wide), HIGH)
    line = pltpu.VMEM((MSG // LANES * devices, LANES), HIGH)
    fields = [height, flux_east, flux_north, bathymetry, wet_mask]

    column_edge = jax.ShapeDtypeStruct((rows, LANES), HIGH)
    edge_spec = pl.BlockSpec((rows, LANES), lambda i: (0, 0))
    west_edge, east_edge = pl.pallas_call(
        column_edge_kernel,
        grid=(1,),
        out_shape=(column_edge,) * 2,
        in_specs=[edge_spec, pl.BlockSpec((rows, LANES), lambda i: (0, cols // LANES - 1))] * 5,
        out_specs=(edge_spec,) * 2,
        compiler_params=small,
        name="column_edges",
    )(*[in_hbm(f) for f in fields for _ in range(2)])
    from_east = shifted(west_edge, "lon", -1)
    from_west = shifted(east_edge, "lon", 1)

    def row_edge(start, keep, after):
        block = [pl.BlockSpec((8, cols), lambda i, at=start // 8 + n: (at, 0)) for n in range(2)]
        ghost = pl.BlockSpec((16, LANES), lambda i: (0, 0))
        return pl.pallas_call(
            lambda *refs: row_edge_kernel(keep, *refs),
            grid=(1,),
            out_shape=jax.ShapeDtypeStruct((64, wide), HIGH),
            in_specs=block * 5 + [ghost, ghost, pl.BlockSpec(memory_space=pl.ANY)],
            out_specs=pl.BlockSpec((64, wide), lambda i: (0, 0)),
            compiler_params=small,
            name="row_edges",
        )(
            *[in_hbm(f) for f in fields for _ in range(2)],
            from_east[start : start + 16],
            from_west[start : start + 16],
            after,
        )

    lane = jnp.arange(wide, dtype=jnp.int32)
    offset = jnp.where(lane < cols + LANES // 2, lane, lane - wide)
    columns = (lax.axis_index("lon") * cols + offset + total_cols) % total_cols
    product = wavenumber[:, None] * columns[None, :] % total_cols
    angle = product.astype(HIGH) * (2.0 * math.pi / total_cols)
    basis = jnp.concatenate([jnp.cos(angle), -jnp.sin(angle)], axis=0)
    weight = (quadrature / math.sqrt(total_cols)).reshape(total_rows // LANES, LANES)
    weight = jnp.pad(weight, ((0, 40 - total_rows // LANES), (0, 0)))
    love = love_factor[None, :]

    sums, table, synth = pl.pallas_call(
        lambda *refs: first_kernel(padded_rows, *refs),
        out_shape=(
            message,
            pltpu.VMEM((cols, LANES), LOW),
            pltpu.VMEM((8 * slots, wide), LOW),
        ),
        in_specs=[VMEM] * 2,
        out_specs=(VMEM,) * 3,
        scratch_shapes=[line],
        compiler_params=small,
        name="first_sums",
    )(height, basis)

    held = pltpu.VMEM((tall, wide), HIGH)
    tiles = pltpu.VMEM((80, LANES), HIGH)
    for step in range(STEPS):
        first, last = step == 0, step == STEPS - 1
        spectral = lax.all_to_all(sums, BOTH, split_axis=0, concat_axis=0, tiled=True)
        if first:
            from_north = shifted_open(row_edge(0, 0, spectral), "lat", -1)
            legendre, turned = pl.pallas_call(
                table_kernel,
                out_shape=(pltpu.VMEM(legendre.shape, LOW), pltpu.VMEM(legendre.shape[::-1], LOW)),
                in_specs=[pl.BlockSpec(memory_space=pl.ANY)] * 2,
                out_specs=(VMEM,) * 2,
                scratch_shapes=[pltpu.SemaphoreType.DMA((total_rows // 256,))],
                compiler_params=small,
                name="tables",
            )(in_hbm(legendre), spectral)
            from_south = shifted_open(row_edge(rows - 16, 16 - HALO, turned), "lat", 1)
        back = pl.pallas_call(
            lambda *refs: legendre_kernel(rows, *refs),
            out_shape=message,
            in_specs=[VMEM] * 5,
            out_specs=VMEM,
            scratch_shapes=[tiles, line],
            compiler_params=small,
            name="legendre_pair",
        )(spectral, *[in_vmem(x) for x in (legendre, weight, love, turned)])
        if first:
            level, east, north, bathy, wet, east_open, north_open = pl.pallas_call(
                assemble_kernel,
                out_shape=(held,) * 7,
                in_specs=[pl.BlockSpec(memory_space=pl.ANY)] * 5 + [VMEM] * 4,
                out_specs=(VMEM,) * 7,
                scratch_shapes=[pltpu.VMEM((rows, cols), jnp.int32), pltpu.SemaphoreType.DMA((5,))],
                compiler_params=small,
                name="assemble",
            )(*[in_hbm(f) for f in fields], from_east, from_west, from_north, from_south)
        bands = lax.all_to_all(back, BOTH, split_axis=0, concat_axis=0, tiled=True)
        operands = [bands] + [
            in_vmem(x) for x in (level, east, north, bathy, wet, east_open, north_open, synth, table)
        ]
        scratch = [pltpu.VMEM((tall + 8, wide), HIGH)] * 3 + [line]
        if last:
            own = jax.ShapeDtypeStruct((rows, cols), HIGH)
            return pl.pallas_call(
                lambda *refs: grid_kernel(padded_rows, True, *refs),
                out_shape=(own,) * 3,
                in_specs=[VMEM] * 9,
                out_specs=(VMEM,) * 3,
                scratch_shapes=scratch,
                compiler_params=small,
                name="grid_last",
            )(*operands[:9])
        level, east, north, sums = pl.pallas_call(
            lambda *refs: grid_kernel(padded_rows, False, *refs),
            out_shape=(field, field, field, message),
            in_specs=[VMEM] * 10,
            out_specs=(VMEM,) * 4,
            scratch_shapes=scratch,
            input_output_aliases={1: 0, 2: 1, 3: 2},
            compiler_params=small,
            name="grid_update",
        )(*operands)


def solution(mesh):
    placed = (
        P("lat", "lon"),
        P("lat", "lon"),
        P("lat", "lon"),
        P("lat", "lon"),
        P("lat", "lon"),
        P(),
        P("lat", None, "lon"),
        P(),
        P("lon"),
    )
    return jax.shard_map(
        shards,
        mesh=mesh,
        in_specs=placed,
        out_specs=(P("lat", "lon"), P("lat", "lon"), P("lat", "lon")),
        check_vma=False,
    )
```

```python
import math

import jax
import jax.numpy as jnp
from jax import lax
from jax.experimental import pallas as pl
from jax.experimental.pallas import tpu as pltpu
from jax.sharding import PartitionSpec as P

STEPS = 12
HALO = STEPS
LANES = 128
SECOND = 192
MSG = 384
SLOT = 16

gravity_step = 0.12
volume_step = 0.12
retain_factor = 0.97

BOTH = ("lat", "lon")
VMEM = pl.BlockSpec(memory_space=pltpu.VMEM)
HIGH = jnp.float32
LOW = jnp.bfloat16


def in_vmem(value):
    return pltpu.with_memory_space_constraint(value, pltpu.VMEM)


def in_hbm(value):
    return pltpu.with_memory_space_constraint(value, pltpu.HBM)


def lanes_of(shape):
    return lax.broadcasted_iota(jnp.int32, shape, 1)


def rows_of(shape):
    return lax.broadcasted_iota(jnp.int32, shape, 0)


def split_pair(value):
    high = value.astype(LOW)
    return high, (value - high.astype(HIGH)).astype(LOW)


def received(got_ref, line_ref):
    every = got_ref.shape[0]
    count = every // 4
    tiles = []
    for tile in range(MSG // LANES):
        base = tile * every
        line_ref[base : base + every, :] = got_ref[:, tile * LANES : (tile + 1) * LANES]
        total = line_ref[pl.ds(base, count, stride=4), :]
        for part in range(1, 4):
            total = total + line_ref[pl.ds(base + part, count, stride=4), :]
        tiles.append(total)
    return jnp.concatenate(tiles, axis=1)


def send(message, out_ref, line_ref):
    every = out_ref.shape[0]
    for tile in range(MSG // LANES):
        base, block = tile * every, slice(tile * LANES, (tile + 1) * LANES)
        for part in range(4):
            line_ref[pl.ds(base + part, every // 4, stride=4), :] = message[:, block]
        out_ref[:, block] = line_ref[base : base + every, :]


def second_part(message):
    return pltpu.roll(message[:, LANES:], 2 * LANES - (SECOND - LANES), 1)


def fourier_sums(rows, read, table_ref, out_ref, line_ref):
    cols = table_ref.shape[0]
    total = jnp.zeros((2 * rows, LANES), HIGH)
    for start in range(0, cols, 256):
        high, low = split_pair(read(start))
        both = jnp.concatenate([high, low], axis=0)
        total = total + jnp.dot(both, table_ref[start : start + 256, :], preferred_element_type=HIGH)
    half = total[:rows] + total[rows:]
    half = half + pltpu.roll(half, LANES // 2, 1)
    half = jnp.concatenate([half, jnp.zeros((256 - rows, LANES), HIGH)], axis=0)
    sums = jnp.transpose(half)
    slots = out_ref.shape[0] // 4
    first = sums[:slots]
    second = pltpu.roll(sums[slots : 2 * slots], SECOND - LANES, 1)
    middle = jnp.where(lanes_of((slots, LANES)) < SECOND - LANES, first[:, LANES:], second[:, :LANES])
    send(jnp.concatenate([first[:, :LANES], middle, second[:, LANES:]], axis=1), out_ref, line_ref)


def first_kernel(rows, height_ref, basis_ref, out_ref, table_ref, synth_ref, line_ref):
    own, cols = height_ref.shape
    basis = basis_ref[...]
    high, low = split_pair(basis)
    count = basis.shape[0]
    synth_ref[:count, :] = high
    synth_ref[count : 2 * count, :] = low
    synth_ref[2 * count : 3 * count, :] = high
    synth_ref[3 * count :, :] = jnp.zeros_like(high)
    for start in range(0, cols, LANES):
        block = slice(start, start + LANES)
        both = jnp.concatenate([high[:, block].astype(HIGH), low[:, block].astype(HIGH)], axis=0)
        table_ref[block, :] = jnp.transpose(both).astype(LOW)

    def read(start):
        block = height_ref[:, start : start + 256]
        return jnp.concatenate([block, jnp.zeros((rows - own, 256), HIGH)], axis=0)

    fourier_sums(rows, read, table_ref, out_ref, line_ref)


def above_of(ref, start, tall):
    if start + 8 < tall:
        return ref[start + 1 : start + 9, :]
    return jnp.concatenate([ref[start + 1 : tall, :], ref[:1, :]], axis=0)


def grid_kernel(rows, last, *refs):
    (got_ref, level_in, east_in, north_in, bathy_ref, wet_ref, east_open_ref, north_open_ref) = refs[:8]
    synth_ref, refs = refs[8], refs[9:]
    if last:
        level_ref, east_ref, north_ref, pot_ref, depth_ref, south_ref, line_ref = refs
    else:
        table_ref, level_ref, east_ref, north_ref, out_ref = refs[:5]
        pot_ref, depth_ref, south_ref, line_ref = refs[5:]
    tall, wide = level_in.shape
    own, cols = level_ref.shape
    message = received(got_ref, line_ref)
    slots = message.shape[0]
    back = jnp.concatenate([message[:, : 2 * LANES], second_part(message)], axis=0)
    back = back * (1.0 / math.sqrt(4 * (wide - LANES)))
    back = jnp.where(
        lanes_of(back.shape) < tall - HALO,
        pltpu.roll(back, 2 * LANES - HALO, 1),
        pltpu.roll(back, tall - HALO, 1),
    )
    high, low = split_pair(back)
    high, low = high.astype(HIGH), low.astype(HIGH)
    stacked = jnp.concatenate([high, high, low, jnp.zeros_like(low)], axis=0)
    factors = jnp.transpose(stacked)[:tall].astype(LOW)
    half_gravity = gravity_step * 0.5
    for start in range(0, wide, 256):
        block = slice(start, min(start + 256, wide))
        pull = jnp.dot(factors, synth_ref[:, block], preferred_element_type=HIGH)
        level = level_in[:, block]
        pot_ref[:tall, block] = level + pull
        depth_ref[:tall, block] = (half_gravity * wet_ref[:, block]) * jnp.maximum(
            bathy_ref[:, block] + level, 0.0
        )
    pot_ref[tall:, :] = pot_ref[:8, :]
    depth_ref[tall:, :] = depth_ref[:8, :]

    def update(start):
        here = slice(start, start + 8)
        above = slice(start + 1, start + 9)
        pot, depth = pot_ref[here, :], depth_ref[here, :]
        pot_east, depth_east = pltpu.roll(pot, wide - 1, 1), pltpu.roll(depth, wide - 1, 1)
        east = east_open_ref[here, :] * (
            east_in[here, :] - (depth + depth_east) * (pot_east - pot)
        )
        north = north_open_ref[here, :] * (
            north_in[here, :] - (depth + depth_ref[above, :]) * (pot_ref[above, :] - pot)
        )
        south_ref[start + 8 : start + 16, :] = north
        below = south_ref[start + 7 : start + 15, :]
        level = level_in[here, :] - (volume_step * wet_ref[here, :]) * (
            east - pltpu.roll(east, 1, 1) + north - below
        )
        if start < own:
            east_ref[here, :] = east[:, :cols]
            north_ref[here, :] = north[:, :cols]
            level_ref[here, :] = level[:, :cols]

    if last:
        update(tall - 8)
        south_ref[:8, :] = south_ref[tall : tall + 8, :]
        for start in range(0, own, 8):
            update(start)
    else:
        seam = tall - 2 * HALO
        south_ref[seam : seam + 8, :] = jnp.zeros((8, wide), HIGH)
        for start in range(seam, tall, 8):
            update(start)
        south_ref[:8, :] = south_ref[tall : tall + 8, :]
        for start in range(0, seam, 8):
            update(start)
        fix = slice(seam, seam + 8)
        row = rows_of((8, wide))
        missed = jnp.where(row == 0, south_ref[seam + 7 : seam + 15, :], 0.0)
        level_ref[fix, :] = level_ref[fix, :] + (volume_step * wet_ref[fix, :]) * missed
        def read(start):
            return level_ref[:rows, start : start + 256]

        fourier_sums(rows, read, table_ref, out_ref, line_ref)


def table_kernel(legendre_ref, unused_ref, held_ref, turned_ref, copies):
    total, degrees = legendre_ref.shape
    chunk = 2 * LANES
    ahead = 8

    def copy(start):
        block = pl.ds(start, chunk)
        return pltpu.make_async_copy(
            legendre_ref.at[block, :], held_ref.at[block, :], copies.at[start // chunk]
        )

    for start in range(0, ahead * chunk, chunk):
        copy(start).start()
    for start in range(0, total, chunk):
        copy(start).wait()
        if start + ahead * chunk < total:
            copy(start + ahead * chunk).start()
        turned_ref[:, start : start + chunk] = jnp.transpose(held_ref[start : start + chunk, :])


def legendre_kernel(
    band, got_ref, legendre_ref, weight_ref, love_ref, turned_ref, out_ref, tiles_ref, line_ref
):
    total, degrees = legendre_ref.shape
    bands = total // band
    chunk = 2 * LANES
    step = band - LANES

    message = received(got_ref, line_ref)
    tall = tiles_ref.shape[0] // 2
    for k, part in enumerate((message[:, :chunk], second_part(message))):
        part = jnp.where(lanes_of(part.shape) < band, part, 0.0)
        part = pltpu.roll(part, 0, 1, stride=step, stride_axis=0)
        early, late = part[:, :LANES], part[:, LANES:]
        zeros = jnp.zeros((tall - bands, LANES), HIGH)
        row = rows_of((tall, LANES))
        early = jnp.concatenate([early, zeros], axis=0)
        late = jnp.concatenate([late, zeros], axis=0)
        wraps = LANES // step
        line = (
            pltpu.roll(late, 1, 0)
            + jnp.where(row < wraps, early, 0.0)
            + jnp.where(row >= wraps + 2, pltpu.roll(early, 2, 0), 0.0)
        )
        tiles_ref[k * tall : (k + 1) * tall, :] = line * weight_ref[...]
    coeff = jnp.zeros((2, degrees), HIGH)
    for start in range(0, total, chunk):
        tile = start // LANES
        weighted = jnp.concatenate(
            [tiles_ref[pl.ds(tile + i, 2, stride=tall), :] for i in range(2)], axis=1
        ).astype(LOW)
        coeff = coeff + jnp.dot(
            weighted, legendre_ref[start : start + chunk, :], preferred_element_type=HIGH
        )
    coeff = jnp.concatenate([coeff * love_ref[...], jnp.zeros((6, degrees), HIGH)], axis=0)
    scaled = coeff.astype(LOW)
    tiles_ref[...] = jnp.zeros_like(tiles_ref)
    for start in range(0, total, chunk):
        back = jnp.dot(
            scaled, turned_ref[:, start : start + chunk], preferred_element_type=HIGH
        )
        row = tall - 2 - start // LANES
        for i in range(2):
            for k in range(2):
                at = k * tall + row - i
                tiles_ref[at : at + 1, :] = back[k : k + 1, i * LANES : (i + 1) * LANES]
    parts = []
    reach = LANES - HALO + step * (bands - 1 - rows_of((bands, LANES)))
    for k in range(2):

        def tile(shift):
            begin = (k + 1) * tall - bands - shift
            return tiles_ref[begin : begin + bands, :]

        window = jnp.concatenate(
            [
                jnp.where(reach < LANES, tile(0), tile(3)),
                jnp.where(reach < 2 * LANES, tile(1), tile(4)),
                tile(2),
            ],
            axis=1,
        )
        shift = (k * SECOND - LANES + HALO - step * (bands - 1)) % MSG
        window = pltpu.roll(window, shift, 1)
        parts.append(pltpu.roll(window, 0, 1, stride=step, stride_axis=0))
    result = jnp.where(lanes_of(parts[0].shape) < SECOND, parts[0], parts[1])
    for index in range(bands):
        at = bands - 1 - index
        out_ref[4 * index : 4 * index + 4, :] = jnp.broadcast_to(result[at : at + 1, :], (4, MSG))


def ghost_tile(index, east, west):
    lane = lanes_of(east.shape)
    east = pltpu.roll(east, LANES - SLOT * index, 1) if index else east
    west = pltpu.roll(west, LANES - SLOT * (index + 1), 1)
    return jnp.where(lane < HALO, east, jnp.where(lane >= LANES - HALO, west, 0.0))


def column_edge_kernel(*refs):
    fields, (west_ref, east_ref) = refs[:-2], refs[-2:]
    lane = lanes_of(west_ref.shape)
    west = jnp.zeros(west_ref.shape, HIGH)
    east = jnp.zeros(east_ref.shape, HIGH)
    for index in range(len(fields) // 2):
        left, right = (ref[...].astype(HIGH) for ref in fields[2 * index : 2 * index + 2])
        here = (lane >= SLOT * index) & (lane < SLOT * (index + 1))
        west = jnp.where(here, pltpu.roll(left, SLOT * index, 1) if index else left, west)
        east = jnp.where(here, pltpu.roll(right, SLOT * (index + 1), 1), east)
    west_ref[...] = west
    east_ref[...] = east


def row_edge_kernel(begin, *refs):
    fields, (from_east, from_west, unused_ref, out_ref) = refs[:-4], refs[-4:]
    cols = fields[0].shape[1]
    keep = slice(begin, begin + HALO)
    out_ref[len(fields) // 2 * HALO :, :] = jnp.zeros_like(out_ref[len(fields) // 2 * HALO :, :])
    for index in range(len(fields) // 2):
        both = jnp.concatenate([ref[...].astype(HIGH) for ref in fields[2 * index : 2 * index + 2]], axis=0)
        where = slice(HALO * index, HALO * (index + 1))
        out_ref[where, :cols] = both[keep]
        out_ref[where, cols:] = ghost_tile(index, from_east[...], from_west[...])[keep]


def assemble_kernel(*refs):
    fields, refs = refs[:5], refs[5:]
    (from_east, from_west, from_north, from_south), refs = refs[:4], refs[4:]
    outs, (east_open_ref, north_open_ref, mask_ref, copies) = refs[:5], refs[5:]
    rows, cols = fields[0].shape
    tall, wide = outs[0].shape
    targets = [out.at[:rows, :cols] for out in outs[:4]] + [mask_ref]
    moves = [
        pltpu.make_async_copy(field, target, copies.at[index])
        for index, (field, target) in enumerate(zip(fields, targets))
    ]
    for move in moves[4:] + moves[:4]:
        move.start()
    for index, out in enumerate(outs):
        out[:rows, cols:] = ghost_tile(index, from_east[...], from_west[...])
        begin = HALO * index
        out[rows:, :] = jnp.concatenate(
            [from_north[begin : begin + HALO, :], from_south[begin : begin + HALO, :]], axis=0
        )
    moves[4].wait()
    wet_ref = outs[4]
    wet_ref[:rows, :cols] = mask_ref[...].astype(HIGH)
    for start in range(0, tall, 8):
        here = slice(start, start + 8)
        wet = wet_ref[here, :]
        above = above_of(wet_ref, start, tall)
        if start <= rows + HALO - 1 < start + 8:
            above = jnp.where(rows_of(above.shape) == rows + HALO - 1 - start, 0.0, above)
        east_open_ref[here, :] = retain_factor * wet * pltpu.roll(wet, wide - 1, 1)
        north_open_ref[here, :] = retain_factor * wet * above
    for move in moves[:4]:
        move.wait()


def shifted(value, axis, by):
    count = lax.axis_size(axis)
    return lax.ppermute(value, axis, [(i, (i + by) % count) for i in range(count)])


def shifted_open(value, axis, by):
    count = lax.axis_size(axis)
    pairs = [(i, i + by) for i in range(count) if 0 <= i + by < count]
    return lax.ppermute(value, axis, pairs)


def shards(
    height,
    flux_east,
    flux_north,
    bathymetry,
    wet_mask,
    wavenumber,
    legendre,
    quadrature,
    love_factor,
):
    lon_count = lax.axis_size("lon")
    lat_count = lax.axis_size("lat")
    rows, cols = height.shape
    slots = wavenumber.shape[0]
    total_cols = cols * lon_count
    total_rows = rows * lat_count
    tall, wide = rows + 2 * HALO, cols + LANES
    devices = lat_count * lon_count
    padded_rows = -(-rows // 16) * 16
    legendre = legendre.reshape(legendre.shape[1:])
    degrees = legendre.shape[1]
    small = pltpu.CompilerParams(vmem_limit_bytes=12 * 2**20)
    message = jax.ShapeDtypeStruct((devices, MSG), HIGH)
    field = jax.ShapeDtypeStruct((tall, wide), HIGH)
    line = pltpu.VMEM((MSG // LANES * devices, LANES), HIGH)
    fields = [height, flux_east, flux_north, bathymetry, wet_mask]

    column_edge = jax.ShapeDtypeStruct((rows, LANES), HIGH)
    edge_spec = pl.BlockSpec((rows, LANES), lambda i: (0, 0))
    west_edge, east_edge = pl.pallas_call(
        column_edge_kernel,
        grid=(1,),
        out_shape=(column_edge,) * 2,
        in_specs=[edge_spec, pl.BlockSpec((rows, LANES), lambda i: (0, cols // LANES - 1))] * 5,
        out_specs=(edge_spec,) * 2,
        compiler_params=small,
        name="column_edges",
    )(*[in_hbm(f) for f in fields for _ in range(2)])
    from_east = shifted(west_edge, "lon", -1)
    from_west = shifted(east_edge, "lon", 1)

    def row_edge(start, keep, after):
        block = [pl.BlockSpec((8, cols), lambda i, at=start // 8 + n: (at, 0)) for n in range(2)]
        ghost = pl.BlockSpec((16, LANES), lambda i: (0, 0))
        return pl.pallas_call(
            lambda *refs: row_edge_kernel(keep, *refs),
            grid=(1,),
            out_shape=jax.ShapeDtypeStruct((64, wide), HIGH),
            in_specs=block * 5 + [ghost, ghost, pl.BlockSpec(memory_space=pl.ANY)],
            out_specs=pl.BlockSpec((64, wide), lambda i: (0, 0)),
            compiler_params=small,
            name="row_edges",
        )(
            *[in_hbm(f) for f in fields for _ in range(2)],
            from_east[start : start + 16],
            from_west[start : start + 16],
            after,
        )

    lane = jnp.arange(wide, dtype=jnp.int32)
    offset = jnp.where(lane < cols + LANES // 2, lane, lane - wide)
    columns = (lax.axis_index("lon") * cols + offset + total_cols) % total_cols
    product = wavenumber[:, None] * columns[None, :] % total_cols
    angle = product.astype(HIGH) * (2.0 * math.pi / total_cols)
    basis = jnp.concatenate([jnp.cos(angle), -jnp.sin(angle)], axis=0)
    weight = (quadrature / math.sqrt(total_cols)).reshape(total_rows // LANES, LANES)
    weight = jnp.pad(weight, ((0, 40 - total_rows // LANES), (0, 0)))
    love = love_factor[None, :]

    sums, table, synth = pl.pallas_call(
        lambda *refs: first_kernel(padded_rows, *refs),
        out_shape=(
            message,
            pltpu.VMEM((cols, LANES), LOW),
            pltpu.VMEM((8 * slots, wide), LOW),
        ),
        in_specs=[VMEM] * 2,
        out_specs=(VMEM,) * 3,
        scratch_shapes=[line],
        compiler_params=small,
        name="first_sums",
    )(height, basis)

    from_north = shifted_open(row_edge(0, 0, sums), "lat", -1)
    held = pltpu.VMEM((tall, wide), HIGH)
    tiles = pltpu.VMEM((80, LANES), HIGH)
    for step in range(STEPS):
        first, last = step == 0, step == STEPS - 1
        spectral = lax.all_to_all(sums, BOTH, split_axis=0, concat_axis=0, tiled=True)
        if first:
            from_south = shifted_open(row_edge(rows - 16, 16 - HALO, spectral), "lat", 1)
            legendre, turned = pl.pallas_call(
                table_kernel,
                out_shape=(pltpu.VMEM(legendre.shape, LOW), pltpu.VMEM(legendre.shape[::-1], LOW)),
                in_specs=[pl.BlockSpec(memory_space=pl.ANY)] * 2,
                out_specs=(VMEM,) * 2,
                scratch_shapes=[pltpu.SemaphoreType.DMA((total_rows // 256,))],
                compiler_params=small,
                name="tables",
            )(in_hbm(legendre), spectral)
        back = pl.pallas_call(
            lambda *refs: legendre_kernel(rows, *refs),
            out_shape=message,
            in_specs=[VMEM] * 5,
            out_specs=VMEM,
            scratch_shapes=[tiles, line],
            compiler_params=small,
            name="legendre_pair",
        )(spectral, *[in_vmem(x) for x in (legendre, weight, love, turned)])
        if first:
            level, east, north, bathy, wet, east_open, north_open = pl.pallas_call(
                assemble_kernel,
                out_shape=(held,) * 7,
                in_specs=[pl.BlockSpec(memory_space=pl.ANY)] * 5 + [VMEM] * 4,
                out_specs=(VMEM,) * 7,
                scratch_shapes=[pltpu.VMEM((rows, cols), jnp.int32), pltpu.SemaphoreType.DMA((5,))],
                compiler_params=small,
                name="assemble",
            )(*[in_hbm(f) for f in fields], from_east, from_west, from_north, from_south)
        bands = lax.all_to_all(back, BOTH, split_axis=0, concat_axis=0, tiled=True)
        operands = [bands] + [
            in_vmem(x) for x in (level, east, north, bathy, wet, east_open, north_open, synth, table)
        ]
        scratch = [pltpu.VMEM((tall + 8, wide), HIGH)] * 3 + [line]
        if last:
            own = jax.ShapeDtypeStruct((rows, cols), HIGH)
            return pl.pallas_call(
                lambda *refs: grid_kernel(padded_rows, True, *refs),
                out_shape=(own,) * 3,
                in_specs=[VMEM] * 9,
                out_specs=(VMEM,) * 3,
                scratch_shapes=scratch,
                compiler_params=small,
                name="grid_last",
            )(*operands[:9])
        level, east, north, sums = pl.pallas_call(
            lambda *refs: grid_kernel(padded_rows, False, *refs),
            out_shape=(field, field, field, message),
            in_specs=[VMEM] * 10,
            out_specs=(VMEM,) * 4,
            scratch_shapes=scratch,
            input_output_aliases={1: 0, 2: 1, 3: 2},
            compiler_params=small,
            name="grid_update",
        )(*operands)


def solution(mesh):
    placed = (
        P("lat", "lon"),
        P("lat", "lon"),
        P("lat", "lon"),
        P("lat", "lon"),
        P("lat", "lon"),
        P(),
        P("lat", None, "lon"),
        P(),
        P("lon"),
    )
    return jax.shard_map(
        shards,
        mesh=mesh,
        in_specs=placed,
        out_specs=(P("lat", "lon"), P("lat", "lon"), P("lat", "lon")),
        check_vma=False,
    )
```

```python
import math

import jax
import jax.numpy as jnp
from jax import lax
from jax.experimental import pallas as pl
from jax.experimental.pallas import tpu as pltpu
from jax.sharding import PartitionSpec as P

STEPS = 12
HALO = STEPS
LANES = 128
SECOND = 192
MSG = 384
LEAVE = 24
SLOT = 16

gravity_step = 0.12
volume_step = 0.12
retain_factor = 0.97

BOTH = ("lat", "lon")
VMEM = pl.BlockSpec(memory_space=pltpu.VMEM)
HIGH = jnp.float32
LOW = jnp.bfloat16


def in_vmem(value):
    return pltpu.with_memory_space_constraint(value, pltpu.VMEM)


def in_hbm(value):
    return pltpu.with_memory_space_constraint(value, pltpu.HBM)


def lanes_of(shape):
    return lax.broadcasted_iota(jnp.int32, shape, 1)


def rows_of(shape):
    return lax.broadcasted_iota(jnp.int32, shape, 0)


def split_pair(value):
    high = value.astype(LOW)
    return high, (value - high.astype(HIGH)).astype(LOW)


def received(got_ref, line_ref):
    every = got_ref.shape[0]
    count = every // 4
    tiles = []
    for tile in range(MSG // LANES):
        base = tile * every
        line_ref[base : base + every, :] = got_ref[:, tile * LANES : (tile + 1) * LANES]
        total = line_ref[pl.ds(base, count, stride=4), :]
        for part in range(1, 4):
            total = total + line_ref[pl.ds(base + part, count, stride=4), :]
        tiles.append(total)
    return jnp.concatenate(tiles, axis=1)


def send(message, out_ref, line_ref):
    every = out_ref.shape[0]
    for tile in range(MSG // LANES):
        base, block = tile * every, slice(tile * LANES, (tile + 1) * LANES)
        for part in range(4):
            line_ref[pl.ds(base + part, every // 4, stride=4), :] = message[:, block]
        out_ref[:, block] = line_ref[base : base + every, :]


def second_part(message):
    return pltpu.roll(message[:, LANES:], 2 * LANES - (SECOND - LANES), 1)


def fourier_sums(rows, read, table_ref, out_ref, line_ref):
    cols = table_ref.shape[0]
    total = jnp.zeros((2 * rows, LANES), HIGH)
    for start in range(0, cols, 256):
        high, low = split_pair(read(start))
        both = jnp.concatenate([high, low], axis=0)
        total = total + jnp.dot(both, table_ref[start : start + 256, :], preferred_element_type=HIGH)
    half = total[:rows] + total[rows:]
    half = half + pltpu.roll(half, LANES // 2, 1)
    half = jnp.concatenate([half, jnp.zeros((256 - rows, LANES), HIGH)], axis=0)
    sums = jnp.transpose(half)
    slots = out_ref.shape[0] // 4
    first = sums[:slots]
    second = pltpu.roll(sums[slots : 2 * slots], SECOND - LANES, 1)
    middle = jnp.where(lanes_of((slots, LANES)) < SECOND - LANES, first[:, LANES:], second[:, :LANES])
    send(jnp.concatenate([first[:, :LANES], middle, second[:, LANES:]], axis=1), out_ref, line_ref)


def first_kernel(rows, height_ref, basis_ref, out_ref, table_ref, synth_ref, line_ref):
    own, cols = height_ref.shape
    basis = basis_ref[...]
    high, low = split_pair(basis)
    count = basis.shape[0]
    synth_ref[:count, :] = high
    synth_ref[count : 2 * count, :] = low
    synth_ref[2 * count : 3 * count, :] = high
    synth_ref[3 * count :, :] = jnp.zeros_like(high)
    for start in range(0, cols, LANES):
        block = slice(start, start + LANES)
        both = jnp.concatenate([high[:, block].astype(HIGH), low[:, block].astype(HIGH)], axis=0)
        table_ref[block, :] = jnp.transpose(both).astype(LOW)

    def read(start):
        block = height_ref[:, start : start + 256]
        return jnp.concatenate([block, jnp.zeros((rows - own, 256), HIGH)], axis=0)

    fourier_sums(rows, read, table_ref, out_ref, line_ref)


def above_of(ref, start, tall):
    if start + 8 < tall:
        return ref[start + 1 : start + 9, :]
    return jnp.concatenate([ref[start + 1 : tall, :], ref[:1, :]], axis=0)


def grid_kernel(rows, last, near, *refs):
    (got_ref, level_in, east_in, north_in, bathy_ref, wet_ref, east_open_ref, north_open_ref) = refs[:8]
    synth_ref, refs = refs[8], refs[9:]
    if last:
        results, refs = refs[:3], refs[3:]
        level_ref, east_ref, north_ref, pot_ref, depth_ref, south_ref, line_ref, copies = refs
    else:
        table_ref, level_ref, east_ref, north_ref, out_ref = refs[:5]
        pot_ref, depth_ref, south_ref, line_ref = refs[5:]
    tall, wide = level_in.shape
    own, cols = level_ref.shape
    message = received(got_ref, line_ref)
    slots = message.shape[0]
    back = jnp.concatenate([message[:, : 2 * LANES], second_part(message)], axis=0)
    back = back * (1.0 / math.sqrt(4 * (wide - LANES)))
    back = jnp.where(
        lanes_of(back.shape) < tall - HALO,
        pltpu.roll(back, 2 * LANES - HALO, 1),
        pltpu.roll(back, tall - HALO, 1),
    )
    high, low = split_pair(back)
    high, low = high.astype(HIGH), low.astype(HIGH)
    stacked = jnp.concatenate([high, high, low, jnp.zeros_like(low)], axis=0)
    factors = jnp.transpose(stacked)[:tall].astype(LOW)
    half_gravity = gravity_step * 0.5
    for start in range(0, wide, 256):
        block = slice(start, min(start + 256, wide))
        pull = jnp.dot(factors, synth_ref[:, block], preferred_element_type=HIGH)
        level = level_in[:, block]
        pot_ref[:tall, block] = level + pull
        depth_ref[:tall, block] = (half_gravity * wet_ref[:, block]) * jnp.maximum(
            bathy_ref[:, block] + level, 0.0
        )
    pot_ref[tall:, :] = pot_ref[:8, :]
    depth_ref[tall:, :] = depth_ref[:8, :]

    def update(start):
        here = slice(start, start + 8)
        above = slice(start + 1, start + 9)
        pot, depth = pot_ref[here, :], depth_ref[here, :]
        pot_east, depth_east = pltpu.roll(pot, wide - 1, 1), pltpu.roll(depth, wide - 1, 1)
        east = east_open_ref[here, :] * (
            east_in[here, :] - (depth + depth_east) * (pot_east - pot)
        )
        north = north_open_ref[here, :] * (
            north_in[here, :] - (depth + depth_ref[above, :]) * (pot_ref[above, :] - pot)
        )
        south_ref[start + 8 : start + 16, :] = north
        below = south_ref[start + 7 : start + 15, :]
        level = level_in[here, :] - (volume_step * wet_ref[here, :]) * (
            east - pltpu.roll(east, 1, 1) + north - below
        )
        if start < own:
            east_ref[here, :] = east[:, :cols]
            north_ref[here, :] = north[:, :cols]
            level_ref[here, :] = level[:, :cols]

    if last:
        update(tall - 8)
        south_ref[:8, :] = south_ref[tall : tall + 8, :]
        moves = []
        begin = 0
        for start in range(0, own, 8):
            update(start)
            end = start + 8
            if end - begin == LEAVE or end == own:
                for index, held in enumerate((level_ref, east_ref, north_ref)):
                    block = pl.ds(begin, end - begin)
                    move = pltpu.make_async_copy(
                        held.at[block, :], results[index].at[block, :], copies.at[len(moves)]
                    )
                    move.start()
                    moves.append(move)
                begin = end
        for move in moves:
            move.wait()
    else:
        seam = tall - 2 * HALO
        south_ref[seam : tall + 8, :] = jnp.zeros((tall + 8 - seam, wide), HIGH)
        for start in (seam, tall - 8) if near else range(seam, tall, 8):
            update(start)
        south_ref[:8, :] = south_ref[tall : tall + 8, :]
        for start in range(0, seam, 8):
            update(start)
        fix = slice(seam, seam + 8)
        row = rows_of((8, wide))
        missed = jnp.where(row == 0, south_ref[seam + 7 : seam + 15, :], 0.0)
        level_ref[fix, :] = level_ref[fix, :] + (volume_step * wet_ref[fix, :]) * missed
        def read(start):
            return level_ref[:rows, start : start + 256]

        fourier_sums(rows, read, table_ref, out_ref, line_ref)


def table_kernel(legendre_ref, unused_ref, held_ref, turned_ref, copies):
    total, degrees = legendre_ref.shape
    chunk = 2 * LANES
    ahead = 8

    def copy(start):
        block = pl.ds(start, chunk)
        return pltpu.make_async_copy(
            legendre_ref.at[block, :], held_ref.at[block, :], copies.at[start // chunk]
        )

    for start in range(0, ahead * chunk, chunk):
        copy(start).start()
    for start in range(0, total, chunk):
        copy(start).wait()
        if start + ahead * chunk < total:
            copy(start + ahead * chunk).start()
        turned_ref[:, start : start + chunk] = jnp.transpose(held_ref[start : start + chunk, :])


def legendre_kernel(
    band, got_ref, legendre_ref, weight_ref, love_ref, turned_ref, out_ref, tiles_ref, line_ref
):
    total, degrees = legendre_ref.shape
    bands = total // band
    chunk = 2 * LANES
    step = band - LANES

    message = received(got_ref, line_ref)
    tall = tiles_ref.shape[0] // 2
    for k, part in enumerate((message[:, :chunk], second_part(message))):
        part = jnp.where(lanes_of(part.shape) < band, part, 0.0)
        part = pltpu.roll(part, 0, 1, stride=step, stride_axis=0)
        early, late = part[:, :LANES], part[:, LANES:]
        zeros = jnp.zeros((tall - bands, LANES), HIGH)
        row = rows_of((tall, LANES))
        early = jnp.concatenate([early, zeros], axis=0)
        late = jnp.concatenate([late, zeros], axis=0)
        wraps = LANES // step
        line = (
            pltpu.roll(late, 1, 0)
            + jnp.where(row < wraps, early, 0.0)
            + jnp.where(row >= wraps + 2, pltpu.roll(early, 2, 0), 0.0)
        )
        tiles_ref[k * tall : (k + 1) * tall, :] = line * weight_ref[...]
    coeff = jnp.zeros((2, degrees), HIGH)
    for start in range(0, total, chunk):
        tile = start // LANES
        weighted = jnp.concatenate(
            [tiles_ref[pl.ds(tile + i, 2, stride=tall), :] for i in range(2)], axis=1
        ).astype(LOW)
        coeff = coeff + jnp.dot(
            weighted, legendre_ref[start : start + chunk, :], preferred_element_type=HIGH
        )
    coeff = jnp.concatenate([coeff * love_ref[...], jnp.zeros((6, degrees), HIGH)], axis=0)
    scaled = coeff.astype(LOW)
    tiles_ref[...] = jnp.zeros_like(tiles_ref)
    for start in range(0, total, chunk):
        back = jnp.dot(
            scaled, turned_ref[:, start : start + chunk], preferred_element_type=HIGH
        )
        row = tall - 2 - start // LANES
        for i in range(2):
            for k in range(2):
                at = k * tall + row - i
                tiles_ref[at : at + 1, :] = back[k : k + 1, i * LANES : (i + 1) * LANES]
    parts = []
    reach = LANES - HALO + step * (bands - 1 - rows_of((bands, LANES)))
    for k in range(2):

        def tile(shift):
            begin = (k + 1) * tall - bands - shift
            return tiles_ref[begin : begin + bands, :]

        window = jnp.concatenate(
            [
                jnp.where(reach < LANES, tile(0), tile(3)),
                jnp.where(reach < 2 * LANES, tile(1), tile(4)),
                tile(2),
            ],
            axis=1,
        )
        shift = (k * SECOND - LANES + HALO - step * (bands - 1)) % MSG
        window = pltpu.roll(window, shift, 1)
        parts.append(pltpu.roll(window, 0, 1, stride=step, stride_axis=0))
    result = jnp.where(lanes_of(parts[0].shape) < SECOND, parts[0], parts[1])
    for index in range(bands):
        at = bands - 1 - index
        out_ref[4 * index : 4 * index + 4, :] = jnp.broadcast_to(result[at : at + 1, :], (4, MSG))


def ghost_tile(index, east, west):
    lane = lanes_of(east.shape)
    east = pltpu.roll(east, LANES - SLOT * index, 1) if index else east
    west = pltpu.roll(west, LANES - SLOT * (index + 1), 1)
    return jnp.where(lane < HALO, east, jnp.where(lane >= LANES - HALO, west, 0.0))


def column_edge_kernel(*refs):
    fields, (west_ref, east_ref) = refs[:-2], refs[-2:]
    lane = lanes_of(west_ref.shape)
    west = jnp.zeros(west_ref.shape, HIGH)
    east = jnp.zeros(east_ref.shape, HIGH)
    for index in range(len(fields) // 2):
        left, right = (ref[...].astype(HIGH) for ref in fields[2 * index : 2 * index + 2])
        here = (lane >= SLOT * index) & (lane < SLOT * (index + 1))
        west = jnp.where(here, pltpu.roll(left, SLOT * index, 1) if index else left, west)
        east = jnp.where(here, pltpu.roll(right, SLOT * (index + 1), 1), east)
    west_ref[...] = west
    east_ref[...] = east


def row_edge_kernel(northern_ref, *refs):
    fields, refs = refs[:-6], refs[-6:]
    east_low, east_high, west_low, west_high, unused_ref, out_ref = refs
    cols = fields[0].shape[1]
    northern = northern_ref[0] == 1

    def keep(low, high):
        both = jnp.concatenate([low, high], axis=0).astype(HIGH)
        return jnp.where(northern, both[16 - HALO :], both[:HALO])

    count = len(fields) // 2
    out_ref[count * HALO :, :] = jnp.zeros_like(out_ref[count * HALO :, :])
    from_east = keep(east_low[...], east_high[...])
    from_west = keep(west_low[...], west_high[...])
    for index in range(count):
        where = slice(HALO * index, HALO * (index + 1))
        out_ref[where, :cols] = keep(fields[2 * index][...], fields[2 * index + 1][...])
        out_ref[where, cols:] = ghost_tile(index, from_east, from_west)


def assemble_kernel(*refs):
    fields, refs = refs[:5], refs[5:]
    (from_east, from_west, early_ref, late_ref, even_ref), refs = refs[:5], refs[5:]
    outs, (east_open_ref, north_open_ref, mask_ref, copies) = refs[:5], refs[5:]
    even = even_ref[0] == 1
    rows, cols = fields[0].shape
    tall, wide = outs[0].shape
    targets = [out.at[:rows, :cols] for out in outs[:4]] + [mask_ref]
    moves = [
        pltpu.make_async_copy(field, target, copies.at[index])
        for index, (field, target) in enumerate(zip(fields, targets))
    ]
    for move in moves[4:] + moves[:4]:
        move.start()
    for index, out in enumerate(outs):
        out[:rows, cols:] = ghost_tile(index, from_east[...], from_west[...])
        begin = HALO * index
        early, late = early_ref[begin : begin + HALO, :], late_ref[begin : begin + HALO, :]
        out[rows:, :] = jnp.concatenate(
            [jnp.where(even, early, late), jnp.where(even, late, early)], axis=0
        )
    moves[4].wait()
    wet_ref = outs[4]
    wet_ref[:rows, :cols] = mask_ref[...].astype(HIGH)
    for start in range(0, tall, 8):
        here = slice(start, start + 8)
        wet = wet_ref[here, :]
        above = above_of(wet_ref, start, tall)
        if start <= rows + HALO - 1 < start + 8:
            above = jnp.where(rows_of(above.shape) == rows + HALO - 1 - start, 0.0, above)
        east_open_ref[here, :] = retain_factor * wet * pltpu.roll(wet, wide - 1, 1)
        north_open_ref[here, :] = retain_factor * wet * above
    for move in moves[:4]:
        move.wait()


def shifted(value, axis, by):
    count = lax.axis_size(axis)
    return lax.ppermute(value, axis, [(i, (i + by) % count) for i in range(count)])


def shards(
    height,
    flux_east,
    flux_north,
    bathymetry,
    wet_mask,
    wavenumber,
    legendre,
    quadrature,
    love_factor,
):
    lon_count = lax.axis_size("lon")
    lat_count = lax.axis_size("lat")
    rows, cols = height.shape
    slots = wavenumber.shape[0]
    total_cols = cols * lon_count
    total_rows = rows * lat_count
    tall, wide = rows + 2 * HALO, cols + LANES
    devices = lat_count * lon_count
    padded_rows = -(-rows // 16) * 16
    legendre = legendre.reshape(legendre.shape[1:])
    degrees = legendre.shape[1]
    small = pltpu.CompilerParams(vmem_limit_bytes=12 * 2**20)
    message = jax.ShapeDtypeStruct((devices, MSG), HIGH)
    field = jax.ShapeDtypeStruct((tall, wide), HIGH)
    line = pltpu.VMEM((MSG // LANES * devices, LANES), HIGH)
    fields = [height, flux_east, flux_north, bathymetry, wet_mask]

    column_edge = jax.ShapeDtypeStruct((rows, LANES), HIGH)
    edge_spec = pl.BlockSpec((rows, LANES), lambda i: (0, 0))
    west_edge, east_edge = pl.pallas_call(
        column_edge_kernel,
        grid=(1,),
        out_shape=(column_edge,) * 2,
        in_specs=[edge_spec, pl.BlockSpec((rows, LANES), lambda i: (0, cols // LANES - 1))] * 5,
        out_specs=(edge_spec,) * 2,
        compiler_params=small,
        name="column_edges",
    )(*[in_hbm(f) for f in fields for _ in range(2)])
    from_east = shifted(west_edge, "lon", -1)
    from_west = shifted(east_edge, "lon", 1)

    even = (1 - lax.axis_index("lat") % 2).astype(jnp.int32).reshape(1)

    def row_edge(northern, after):
        def end(width, n):
            return pl.BlockSpec((8, width), lambda i, flag: (flag[0] * (rows // 8 - 2) + n, 0))

        return pl.pallas_call(
            row_edge_kernel,
            grid_spec=pltpu.PrefetchScalarGridSpec(
                num_scalar_prefetch=1,
                grid=(1,),
                in_specs=[end(cols, 0), end(cols, 1)] * 5
                + [end(LANES, 0), end(LANES, 1)] * 2
                + [pl.BlockSpec(memory_space=pl.ANY)],
                out_specs=pl.BlockSpec((64, wide), lambda i, flag: (0, 0)),
            ),
            out_shape=jax.ShapeDtypeStruct((64, wide), HIGH),
            compiler_params=small,
            name="row_edges",
        )(
            northern,
            *[in_hbm(f) for f in fields for _ in range(2)],
            from_east,
            from_east,
            from_west,
            from_west,
            after,
        )

    def swapped(value, begin):
        count = lat_count
        pairs = [(i, i + 1) for i in range(begin, count - 1, 2)]
        return lax.ppermute(value, "lat", pairs + [(j, i) for i, j in pairs])

    lane = jnp.arange(wide, dtype=jnp.int32)
    offset = jnp.where(lane < cols + LANES // 2, lane, lane - wide)
    columns = (lax.axis_index("lon") * cols + offset + total_cols) % total_cols
    product = wavenumber[:, None] * columns[None, :] % total_cols
    angle = product.astype(HIGH) * (2.0 * math.pi / total_cols)
    basis = jnp.concatenate([jnp.cos(angle), -jnp.sin(angle)], axis=0)
    weight = (quadrature / math.sqrt(total_cols)).reshape(total_rows // LANES, LANES)
    weight = jnp.pad(weight, ((0, 40 - total_rows // LANES), (0, 0)))
    love = love_factor[None, :]

    sums, table, synth = pl.pallas_call(
        lambda *refs: first_kernel(padded_rows, *refs),
        out_shape=(
            message,
            pltpu.VMEM((cols, LANES), LOW),
            pltpu.VMEM((8 * slots, wide), LOW),
        ),
        in_specs=[VMEM] * 2,
        out_specs=(VMEM,) * 3,
        scratch_shapes=[line],
        compiler_params=small,
        name="first_sums",
    )(height, basis)

    early = swapped(row_edge(even, sums), 0)
    held = pltpu.VMEM((tall, wide), HIGH)
    tiles = pltpu.VMEM((80, LANES), HIGH)
    for step in range(STEPS):
        first, last = step == 0, step == STEPS - 1
        spectral = lax.all_to_all(sums, BOTH, split_axis=0, concat_axis=0, tiled=True)
        if first:
            late = swapped(row_edge(1 - even, spectral), 1)
            legendre, turned = pl.pallas_call(
                table_kernel,
                out_shape=(pltpu.VMEM(legendre.shape, LOW), pltpu.VMEM(legendre.shape[::-1], LOW)),
                in_specs=[pl.BlockSpec(memory_space=pl.ANY)] * 2,
                out_specs=(VMEM,) * 2,
                scratch_shapes=[pltpu.SemaphoreType.DMA((total_rows // 256,))],
                compiler_params=small,
                name="tables",
            )(in_hbm(legendre), spectral)
        back = pl.pallas_call(
            lambda *refs: legendre_kernel(rows, *refs),
            out_shape=message,
            in_specs=[VMEM] * 5,
            out_specs=VMEM,
            scratch_shapes=[tiles, line],
            compiler_params=small,
            name="legendre_pair",
        )(spectral, *[in_vmem(x) for x in (legendre, weight, love, turned)])
        if first:
            level, east, north, bathy, wet, east_open, north_open = pl.pallas_call(
                assemble_kernel,
                out_shape=(held,) * 7,
                in_specs=[pl.BlockSpec(memory_space=pl.ANY)] * 5
                + [VMEM] * 4
                + [pl.BlockSpec(memory_space=pltpu.SMEM)],
                out_specs=(VMEM,) * 7,
                scratch_shapes=[pltpu.VMEM((rows, cols), jnp.int32), pltpu.SemaphoreType.DMA((5,))],
                compiler_params=small,
                name="assemble",
            )(*[in_hbm(f) for f in fields], from_east, from_west, early, late, even)
        bands = lax.all_to_all(back, BOTH, split_axis=0, concat_axis=0, tiled=True)
        operands = [bands] + [
            in_vmem(x) for x in (level, east, north, bathy, wet, east_open, north_open, synth, table)
        ]
        scratch = [pltpu.VMEM((tall + 8, wide), HIGH)] * 3 + [line]
        if last:
            own = jax.ShapeDtypeStruct((rows, cols), HIGH)
            return pl.pallas_call(
                lambda *refs: grid_kernel(padded_rows, True, True, *refs),
                out_shape=(own,) * 3,
                in_specs=[VMEM] * 9,
                out_specs=(pl.BlockSpec(memory_space=pl.ANY),) * 3,
                scratch_shapes=[pltpu.VMEM((rows, cols), HIGH)] * 3
                + scratch
                + [pltpu.SemaphoreType.DMA((3 * -(-rows // LEAVE),))],
                compiler_params=small,
                name="grid_last",
            )(*operands[:9])
        level, east, north, sums = pl.pallas_call(
            lambda *refs, near=STEPS - 1 - step < 8: grid_kernel(padded_rows, False, near, *refs),
            out_shape=(field, field, field, message),
            in_specs=[VMEM] * 10,
            out_specs=(VMEM,) * 4,
            scratch_shapes=scratch,
            input_output_aliases={1: 0, 2: 1, 3: 2},
            compiler_params=small,
            name="grid_update",
        )(*operands)


def solution(mesh):
    placed = (
        P("lat", "lon"),
        P("lat", "lon"),
        P("lat", "lon"),
        P("lat", "lon"),
        P("lat", "lon"),
        P(),
        P("lat", None, "lon"),
        P(),
        P("lon"),
    )
    return jax.shard_map(
        shards,
        mesh=mesh,
        in_specs=placed,
        out_specs=(P("lat", "lon"), P("lat", "lon"), P("lat", "lon")),
        check_vma=False,
    )
```

```python
import math

import jax
import jax.numpy as jnp
from jax import lax
from jax.experimental import pallas as pl
from jax.experimental.pallas import tpu as pltpu
from jax.sharding import PartitionSpec as P

STEPS = 12
HALO = STEPS
LANES = 128
SECOND = 192
MSG = 384
LEAVE = 24
SLOT = 16

gravity_step = 0.12
volume_step = 0.12
retain_factor = 0.97

BOTH = ("lat", "lon")
VMEM = pl.BlockSpec(memory_space=pltpu.VMEM)
HIGH = jnp.float32
LOW = jnp.bfloat16


def in_vmem(value):
    return pltpu.with_memory_space_constraint(value, pltpu.VMEM)


def in_hbm(value):
    return pltpu.with_memory_space_constraint(value, pltpu.HBM)


def lanes_of(shape):
    return lax.broadcasted_iota(jnp.int32, shape, 1)


def rows_of(shape):
    return lax.broadcasted_iota(jnp.int32, shape, 0)


def split_pair(value):
    high = value.astype(LOW)
    return high, (value - high.astype(HIGH)).astype(LOW)


def received(got_ref, line_ref):
    every = got_ref.shape[0]
    count = every // 4
    tiles = []
    for tile in range(MSG // LANES):
        base = tile * every
        line_ref[base : base + every, :] = got_ref[:, tile * LANES : (tile + 1) * LANES]
        total = line_ref[pl.ds(base, count, stride=4), :]
        for part in range(1, 4):
            total = total + line_ref[pl.ds(base + part, count, stride=4), :]
        tiles.append(total)
    return jnp.concatenate(tiles, axis=1)


def send(message, out_ref, line_ref):
    every = out_ref.shape[0]
    for tile in range(MSG // LANES):
        base, block = tile * every, slice(tile * LANES, (tile + 1) * LANES)
        for part in range(4):
            line_ref[pl.ds(base + part, every // 4, stride=4), :] = message[:, block]
        out_ref[:, 0, block] = line_ref[base : base + every, :]


def second_part(message):
    return pltpu.roll(message[:, LANES:], 2 * LANES - (SECOND - LANES), 1)


def fourier_sums(rows, read, table_ref, out_ref, line_ref):
    cols = table_ref.shape[0]
    total = jnp.zeros((2 * rows, LANES), HIGH)
    for start in range(0, cols, 256):
        high, low = split_pair(read(start))
        both = jnp.concatenate([high, low], axis=0)
        total = total + jnp.dot(both, table_ref[start : start + 256, :], preferred_element_type=HIGH)
    half = total[:rows] + total[rows:]
    half = half + pltpu.roll(half, LANES // 2, 1)
    half = jnp.concatenate([half, jnp.zeros((256 - rows, LANES), HIGH)], axis=0)
    sums = jnp.transpose(half)
    slots = out_ref.shape[0] // 4
    first = sums[:slots]
    second = pltpu.roll(sums[slots : 2 * slots], SECOND - LANES, 1)
    middle = jnp.where(lanes_of((slots, LANES)) < SECOND - LANES, first[:, LANES:], second[:, :LANES])
    send(jnp.concatenate([first[:, :LANES], middle, second[:, LANES:]], axis=1), out_ref, line_ref)


def first_kernel(rows, height_ref, basis_ref, out_ref, table_ref, synth_ref, line_ref):
    own, cols = height_ref.shape
    basis = basis_ref[...]
    high, low = split_pair(basis)
    count = basis.shape[0]
    synth_ref[:count, :] = high
    synth_ref[count : 2 * count, :] = low
    synth_ref[2 * count : 3 * count, :] = high
    synth_ref[3 * count :, :] = jnp.zeros_like(high)
    for start in range(0, cols, LANES):
        block = slice(start, start + LANES)
        both = jnp.concatenate([high[:, block].astype(HIGH), low[:, block].astype(HIGH)], axis=0)
        table_ref[block, :] = jnp.transpose(both).astype(LOW)

    def read(start):
        block = height_ref[:, start : start + 256]
        return jnp.concatenate([block, jnp.zeros((rows - own, 256), HIGH)], axis=0)

    fourier_sums(rows, read, table_ref, out_ref, line_ref)


def above_of(ref, start, tall):
    if start + 8 < tall:
        return ref[start + 1 : start + 9, :]
    return jnp.concatenate([ref[start + 1 : tall, :], ref[:1, :]], axis=0)


def grid_kernel(rows, last, near, *refs):
    (got_ref, level_in, east_in, north_in, bathy_ref, wet_ref, east_open_ref, north_open_ref) = refs[:8]
    synth_ref, refs = refs[8], refs[9:]
    if last:
        results, refs = refs[:3], refs[3:]
        level_ref, east_ref, north_ref, pot_ref, depth_ref, south_ref, line_ref, copies = refs
    else:
        table_ref, level_ref, east_ref, north_ref, out_ref = refs[:5]
        pot_ref, depth_ref, south_ref, line_ref = refs[5:]
    tall, wide = level_in.shape
    own, cols = level_ref.shape
    message = received(got_ref, line_ref)
    slots = message.shape[0]
    back = jnp.concatenate([message[:, : 2 * LANES], second_part(message)], axis=0)
    back = back * (1.0 / math.sqrt(4 * (wide - LANES)))
    back = jnp.where(
        lanes_of(back.shape) < tall - HALO,
        pltpu.roll(back, 2 * LANES - HALO, 1),
        pltpu.roll(back, tall - HALO, 1),
    )
    high, low = split_pair(back)
    high, low = high.astype(HIGH), low.astype(HIGH)
    stacked = jnp.concatenate([high, high, low, jnp.zeros_like(low)], axis=0)
    factors = jnp.transpose(stacked)[:tall].astype(LOW)
    half_gravity = gravity_step * 0.5
    for start in range(0, wide, 256):
        block = slice(start, min(start + 256, wide))
        pull = jnp.dot(factors, synth_ref[:, block], preferred_element_type=HIGH)
        level = level_in[:, block]
        pot_ref[:tall, block] = level + pull
        depth_ref[:tall, block] = (half_gravity * wet_ref[:, block]) * jnp.maximum(
            bathy_ref[:, block] + level, 0.0
        )
    pot_ref[tall:, :] = pot_ref[:8, :]
    depth_ref[tall:, :] = depth_ref[:8, :]

    def update(start):
        here = slice(start, start + 8)
        above = slice(start + 1, start + 9)
        pot, depth = pot_ref[here, :], depth_ref[here, :]
        pot_east, depth_east = pltpu.roll(pot, wide - 1, 1), pltpu.roll(depth, wide - 1, 1)
        east = east_open_ref[here, :] * (
            east_in[here, :] - (depth + depth_east) * (pot_east - pot)
        )
        north = north_open_ref[here, :] * (
            north_in[here, :] - (depth + depth_ref[above, :]) * (pot_ref[above, :] - pot)
        )
        south_ref[start + 8 : start + 16, :] = north
        below = south_ref[start + 7 : start + 15, :]
        level = level_in[here, :] - (volume_step * wet_ref[here, :]) * (
            east - pltpu.roll(east, 1, 1) + north - below
        )
        if start < own:
            east_ref[here, :] = east[:, :cols]
            north_ref[here, :] = north[:, :cols]
            level_ref[here, :] = level[:, :cols]

    if last:
        update(tall - 8)
        south_ref[:8, :] = south_ref[tall : tall + 8, :]
        moves = []
        begin = 0
        for start in range(0, own, 8):
            update(start)
            end = start + 8
            if end - begin == LEAVE or end == own:
                for index, held in enumerate((level_ref, east_ref, north_ref)):
                    block = pl.ds(begin, end - begin)
                    move = pltpu.make_async_copy(
                        held.at[block, :], results[index].at[block, :], copies.at[len(moves)]
                    )
                    move.start()
                    moves.append(move)
                begin = end
        for move in moves:
            move.wait()
    else:
        seam = tall - 2 * HALO
        south_ref[seam : tall + 8, :] = jnp.zeros((tall + 8 - seam, wide), HIGH)
        for start in (seam, tall - 8) if near else range(seam, tall, 8):
            update(start)
        south_ref[:8, :] = south_ref[tall : tall + 8, :]
        for start in range(0, seam, 8):
            update(start)
        fix = slice(seam, seam + 8)
        row = rows_of((8, wide))
        missed = jnp.where(row == 0, south_ref[seam + 7 : seam + 15, :], 0.0)
        level_ref[fix, :] = level_ref[fix, :] + (volume_step * wet_ref[fix, :]) * missed
        def read(start):
            return level_ref[:rows, start : start + 256]

        fourier_sums(rows, read, table_ref, out_ref, line_ref)


def table_kernel(legendre_ref, unused_ref, held_ref, turned_ref, copies):
    total, degrees = legendre_ref.shape
    chunk = 2 * LANES
    ahead = 8

    def copy(start):
        block = pl.ds(start, chunk)
        return pltpu.make_async_copy(
            legendre_ref.at[block, :], held_ref.at[block, :], copies.at[start // chunk]
        )

    for start in range(0, ahead * chunk, chunk):
        copy(start).start()
    for start in range(0, total, chunk):
        copy(start).wait()
        if start + ahead * chunk < total:
            copy(start + ahead * chunk).start()
        turned_ref[:, start : start + chunk] = jnp.transpose(held_ref[start : start + chunk, :])


def legendre_kernel(
    band, got_ref, legendre_ref, weight_ref, love_ref, turned_ref, out_ref, tiles_ref, line_ref
):
    total, degrees = legendre_ref.shape
    bands = total // band
    chunk = 2 * LANES
    step = band - LANES

    message = received(got_ref, line_ref)
    tall = tiles_ref.shape[0] // 2
    for k, part in enumerate((message[:, :chunk], second_part(message))):
        part = jnp.where(lanes_of(part.shape) < band, part, 0.0)
        part = pltpu.roll(part, 0, 1, stride=step, stride_axis=0)
        early, late = part[:, :LANES], part[:, LANES:]
        zeros = jnp.zeros((tall - bands, LANES), HIGH)
        row = rows_of((tall, LANES))
        early = jnp.concatenate([early, zeros], axis=0)
        late = jnp.concatenate([late, zeros], axis=0)
        wraps = LANES // step
        line = (
            pltpu.roll(late, 1, 0)
            + jnp.where(row < wraps, early, 0.0)
            + jnp.where(row >= wraps + 2, pltpu.roll(early, 2, 0), 0.0)
        )
        tiles_ref[k * tall : (k + 1) * tall, :] = line * weight_ref[...]
    coeff = jnp.zeros((2, degrees), HIGH)
    for start in range(0, total, chunk):
        tile = start // LANES
        weighted = jnp.concatenate(
            [tiles_ref[pl.ds(tile + i, 2, stride=tall), :] for i in range(2)], axis=1
        ).astype(LOW)
        coeff = coeff + jnp.dot(
            weighted, legendre_ref[start : start + chunk, :], preferred_element_type=HIGH
        )
    coeff = jnp.concatenate([coeff * love_ref[...], jnp.zeros((6, degrees), HIGH)], axis=0)
    scaled = coeff.astype(LOW)
    tiles_ref[...] = jnp.zeros_like(tiles_ref)
    for start in range(0, total, chunk):
        back = jnp.dot(
            scaled, turned_ref[:, start : start + chunk], preferred_element_type=HIGH
        )
        row = tall - 2 - start // LANES
        for i in range(2):
            for k in range(2):
                at = k * tall + row - i
                tiles_ref[at : at + 1, :] = back[k : k + 1, i * LANES : (i + 1) * LANES]
    parts = []
    reach = LANES - HALO + step * (bands - 1 - rows_of((bands, LANES)))
    for k in range(2):

        def tile(shift):
            begin = (k + 1) * tall - bands - shift
            return tiles_ref[begin : begin + bands, :]

        window = jnp.concatenate(
            [
                jnp.where(reach < LANES, tile(0), tile(3)),
                jnp.where(reach < 2 * LANES, tile(1), tile(4)),
                tile(2),
            ],
            axis=1,
        )
        shift = (k * SECOND - LANES + HALO - step * (bands - 1)) % MSG
        window = pltpu.roll(window, shift, 1)
        parts.append(pltpu.roll(window, 0, 1, stride=step, stride_axis=0))
    result = jnp.where(lanes_of(parts[0].shape) < SECOND, parts[0], parts[1])
    for index in range(bands):
        at = bands - 1 - index
        out_ref[4 * index : 4 * index + 4, 0, :] = jnp.broadcast_to(result[at : at + 1, :], (4, MSG))


def ghost_tile(index, east, west):
    lane = lanes_of(east.shape)
    east = pltpu.roll(east, LANES - SLOT * index, 1) if index else east
    west = pltpu.roll(west, LANES - SLOT * (index + 1), 1)
    return jnp.where(lane < HALO, east, jnp.where(lane >= LANES - HALO, west, 0.0))


def column_edge_kernel(*refs):
    fields, (west_ref, east_ref) = refs[:-2], refs[-2:]
    lane = lanes_of(west_ref.shape)
    west = jnp.zeros(west_ref.shape, HIGH)
    east = jnp.zeros(east_ref.shape, HIGH)
    for index in range(len(fields) // 2):
        left, right = (ref[...].astype(HIGH) for ref in fields[2 * index : 2 * index + 2])
        here = (lane >= SLOT * index) & (lane < SLOT * (index + 1))
        west = jnp.where(here, pltpu.roll(left, SLOT * index, 1) if index else left, west)
        east = jnp.where(here, pltpu.roll(right, SLOT * (index + 1), 1), east)
    west_ref[...] = west
    east_ref[...] = east


def row_edge_kernel(northern_ref, *refs):
    fields, refs = refs[:-6], refs[-6:]
    east_low, east_high, west_low, west_high, unused_ref, out_ref = refs
    cols = fields[0].shape[1]
    northern = northern_ref[0] == 1

    def keep(low, high):
        both = jnp.concatenate([low, high], axis=0).astype(HIGH)
        return jnp.where(northern, both[16 - HALO :], both[:HALO])

    count = len(fields) // 2
    out_ref[count * HALO :, :] = jnp.zeros_like(out_ref[count * HALO :, :])
    from_east = keep(east_low[...], east_high[...])
    from_west = keep(west_low[...], west_high[...])
    for index in range(count):
        where = slice(HALO * index, HALO * (index + 1))
        out_ref[where, :cols] = keep(fields[2 * index][...], fields[2 * index + 1][...])
        out_ref[where, cols:] = ghost_tile(index, from_east, from_west)


def assemble_kernel(*refs):
    fields, refs = refs[:5], refs[5:]
    (from_east, from_west, early_ref, late_ref, even_ref), refs = refs[:5], refs[5:]
    outs, (east_open_ref, north_open_ref, mask_ref, copies) = refs[:5], refs[5:]
    even = even_ref[0] == 1
    rows, cols = fields[0].shape
    tall, wide = outs[0].shape
    targets = [out.at[:rows, :cols] for out in outs[:4]] + [mask_ref]
    moves = [
        pltpu.make_async_copy(field, target, copies.at[index])
        for index, (field, target) in enumerate(zip(fields, targets))
    ]
    for move in moves[4:] + moves[:4]:
        move.start()
    for index, out in enumerate(outs):
        out[:rows, cols:] = ghost_tile(index, from_east[...], from_west[...])
        begin = HALO * index
        early, late = early_ref[begin : begin + HALO, :], late_ref[begin : begin + HALO, :]
        out[rows:, :] = jnp.concatenate(
            [jnp.where(even, early, late), jnp.where(even, late, early)], axis=0
        )
    moves[4].wait()
    wet_ref = outs[4]
    wet_ref[:rows, :cols] = mask_ref[...].astype(HIGH)
    for start in range(0, tall, 8):
        here = slice(start, start + 8)
        wet = wet_ref[here, :]
        above = above_of(wet_ref, start, tall)
        if start <= rows + HALO - 1 < start + 8:
            above = jnp.where(rows_of(above.shape) == rows + HALO - 1 - start, 0.0, above)
        east_open_ref[here, :] = retain_factor * wet * pltpu.roll(wet, wide - 1, 1)
        north_open_ref[here, :] = retain_factor * wet * above
    for move in moves[:4]:
        move.wait()


def shifted(value, axis, by):
    count = lax.axis_size(axis)
    return lax.ppermute(value, axis, [(i, (i + by) % count) for i in range(count)])


def shards(
    height,
    flux_east,
    flux_north,
    bathymetry,
    wet_mask,
    wavenumber,
    legendre,
    quadrature,
    love_factor,
):
    lon_count = lax.axis_size("lon")
    lat_count = lax.axis_size("lat")
    rows, cols = height.shape
    slots = wavenumber.shape[0]
    total_cols = cols * lon_count
    total_rows = rows * lat_count
    tall, wide = rows + 2 * HALO, cols + LANES
    devices = lat_count * lon_count
    padded_rows = -(-rows // 16) * 16
    legendre = legendre.reshape(legendre.shape[1:])
    degrees = legendre.shape[1]
    small = pltpu.CompilerParams(vmem_limit_bytes=12 * 2**20)
    message = jax.ShapeDtypeStruct((devices, 1, MSG), HIGH)
    field = jax.ShapeDtypeStruct((tall, wide), HIGH)
    line = pltpu.VMEM((MSG // LANES * devices, LANES), HIGH)
    fields = [height, flux_east, flux_north, bathymetry, wet_mask]

    column_edge = jax.ShapeDtypeStruct((rows, LANES), HIGH)
    edge_spec = pl.BlockSpec((rows, LANES), lambda i: (0, 0))
    west_edge, east_edge = pl.pallas_call(
        column_edge_kernel,
        grid=(1,),
        out_shape=(column_edge,) * 2,
        in_specs=[edge_spec, pl.BlockSpec((rows, LANES), lambda i: (0, cols // LANES - 1))] * 5,
        out_specs=(edge_spec,) * 2,
        compiler_params=small,
        name="column_edges",
    )(*[in_hbm(f) for f in fields for _ in range(2)])
    from_east = shifted(west_edge, "lon", -1)
    from_west = shifted(east_edge, "lon", 1)

    even = (1 - lax.axis_index("lat") % 2).astype(jnp.int32).reshape(1)

    def row_edge(northern, after):
        def end(width, n):
            return pl.BlockSpec((8, width), lambda i, flag: (flag[0] * (rows // 8 - 2) + n, 0))

        return pl.pallas_call(
            row_edge_kernel,
            grid_spec=pltpu.PrefetchScalarGridSpec(
                num_scalar_prefetch=1,
                grid=(1,),
                in_specs=[end(cols, 0), end(cols, 1)] * 5
                + [end(LANES, 0), end(LANES, 1)] * 2
                + [pl.BlockSpec(memory_space=pl.ANY)],
                out_specs=pl.BlockSpec((64, wide), lambda i, flag: (0, 0)),
            ),
            out_shape=jax.ShapeDtypeStruct((64, wide), HIGH),
            compiler_params=small,
            name="row_edges",
        )(
            northern,
            *[in_hbm(f) for f in fields for _ in range(2)],
            from_east,
            from_east,
            from_west,
            from_west,
            after,
        )

    def swapped(value, begin):
        count = lat_count
        pairs = [(i, i + 1) for i in range(begin, count - 1, 2)]
        return lax.ppermute(value, "lat", pairs + [(j, i) for i, j in pairs])

    lane = jnp.arange(wide, dtype=jnp.int32)
    offset = jnp.where(lane < cols + LANES // 2, lane, lane - wide)
    columns = (lax.axis_index("lon") * cols + offset + total_cols) % total_cols
    product = wavenumber[:, None] * columns[None, :] % total_cols
    angle = product.astype(HIGH) * (2.0 * math.pi / total_cols)
    basis = jnp.concatenate([jnp.cos(angle), -jnp.sin(angle)], axis=0)
    weight = (quadrature / math.sqrt(total_cols)).reshape(total_rows // LANES, LANES)
    weight = jnp.pad(weight, ((0, 40 - total_rows // LANES), (0, 0)))
    love = love_factor[None, :]

    sums, table, synth = pl.pallas_call(
        lambda *refs: first_kernel(padded_rows, *refs),
        out_shape=(
            message,
            pltpu.VMEM((cols, LANES), LOW),
            pltpu.VMEM((8 * slots, wide), LOW),
        ),
        in_specs=[VMEM] * 2,
        out_specs=(VMEM,) * 3,
        scratch_shapes=[line],
        compiler_params=small,
        name="first_sums",
    )(height, basis)

    early = swapped(row_edge(even, sums), 0)
    held = pltpu.VMEM((tall, wide), HIGH)
    tiles = pltpu.VMEM((80, LANES), HIGH)
    for step in range(STEPS):
        first, last = step == 0, step == STEPS - 1
        spectral = lax.all_to_all(sums, BOTH, split_axis=0, concat_axis=0, tiled=True)[:, 0]
        if first:
            late = swapped(row_edge(1 - even, spectral), 1)
            legendre, turned = pl.pallas_call(
                table_kernel,
                out_shape=(pltpu.VMEM(legendre.shape, LOW), pltpu.VMEM(legendre.shape[::-1], LOW)),
                in_specs=[pl.BlockSpec(memory_space=pl.ANY)] * 2,
                out_specs=(VMEM,) * 2,
                scratch_shapes=[pltpu.SemaphoreType.DMA((total_rows // 256,))],
                compiler_params=small,
                name="tables",
            )(in_hbm(legendre), spectral)
        back = pl.pallas_call(
            lambda *refs: legendre_kernel(rows, *refs),
            out_shape=message,
            in_specs=[VMEM] * 5,
            out_specs=VMEM,
            scratch_shapes=[tiles, line],
            compiler_params=small,
            name="legendre_pair",
        )(spectral, *[in_vmem(x) for x in (legendre, weight, love, turned)])
        if first:
            level, east, north, bathy, wet, east_open, north_open = pl.pallas_call(
                assemble_kernel,
                out_shape=(held,) * 7,
                in_specs=[pl.BlockSpec(memory_space=pl.ANY)] * 5
                + [VMEM] * 4
                + [pl.BlockSpec(memory_space=pltpu.SMEM)],
                out_specs=(VMEM,) * 7,
                scratch_shapes=[pltpu.VMEM((rows, cols), jnp.int32), pltpu.SemaphoreType.DMA((5,))],
                compiler_params=small,
                name="assemble",
            )(*[in_hbm(f) for f in fields], from_east, from_west, early, late, even)
        bands = lax.all_to_all(back, BOTH, split_axis=0, concat_axis=0, tiled=True)[:, 0]
        operands = [bands] + [
            in_vmem(x) for x in (level, east, north, bathy, wet, east_open, north_open, synth, table)
        ]
        scratch = [pltpu.VMEM((tall + 8, wide), HIGH)] * 3 + [line]
        if last:
            own = jax.ShapeDtypeStruct((rows, cols), HIGH)
            return pl.pallas_call(
                lambda *refs: grid_kernel(padded_rows, True, True, *refs),
                out_shape=(own,) * 3,
                in_specs=[VMEM] * 9,
                out_specs=(pl.BlockSpec(memory_space=pl.ANY),) * 3,
                scratch_shapes=[pltpu.VMEM((rows, cols), HIGH)] * 3
                + scratch
                + [pltpu.SemaphoreType.DMA((3 * -(-rows // LEAVE),))],
                compiler_params=small,
                name="grid_last",
            )(*operands[:9])
        level, east, north, sums = pl.pallas_call(
            lambda *refs, near=STEPS - 1 - step < 8: grid_kernel(padded_rows, False, near, *refs),
            out_shape=(field, field, field, message),
            in_specs=[VMEM] * 10,
            out_specs=(VMEM,) * 4,
            scratch_shapes=scratch,
            input_output_aliases={1: 0, 2: 1, 3: 2},
            compiler_params=small,
            name="grid_update",
        )(*operands)


def solution(mesh):
    placed = (
        P("lat", "lon"),
        P("lat", "lon"),
        P("lat", "lon"),
        P("lat", "lon"),
        P("lat", "lon"),
        P(),
        P("lat", None, "lon"),
        P(),
        P("lon"),
    )
    return jax.shard_map(
        shards,
        mesh=mesh,
        in_specs=placed,
        out_specs=(P("lat", "lon"), P("lat", "lon"), P("lat", "lon")),
        check_vma=False,
    )
```
